32 devices in a mesh: row: 8 (over z, x), col: 4 (over y, core).
Axes of the slice: x: 2, y: 2, z: 4, core: 2. Of those that a mesh axis runs over, the one named last changes fastest.
Arguments:
- panel: float32 [256, 16384], P('col', 'row'), may hold values from -6 to 6
- cauchy: float32 [256, 256], replicated, may hold values from -1 to 1
- refl_v: float32 [2, 128, 256, 128], P(None, 'row'), may hold values from -1 to 1
- block_start: int32 [2], replicated, may hold values from 0 to 127
Outputs:
- eigvec_out: float32 [256, 16384], P('col', 'row')
The draws below stay inside these ranges and needn't reach their ends.
All inputs are finite; a program needn't handle non-finite values.
Results may differ from the reference program's by a relative error of at most 0.0003.
Values sent between devices are 32-bit elements; how exact they have to be, the bound alone decides.
No kernel may reach another device: no remote copies, remote signals or barrier semaphores. Data moves between devices by JAX's collectives and lax.ppermute only.
A program may use at most 128 MiB of HBM per device.

```python
import math
import jax
import jax.numpy as jnp
from jax import lax

HALF_WIDTH = 128
P_SIZE = 256
PASS_TOTAL = 2
N = 16384
PIECES_PER_PASS = 128


def draw_cauchy(key, part):
    seeded_generators = jax.random.split(jax.random.fold_in(key, 23), 4)
    jitter = jax.random.uniform(seeded_generators[0], (P_SIZE,), jnp.float32, -0.3, 0.3)
    pole_set = jnp.arange(P_SIZE, dtype=jnp.float32) + jitter
    spacing = jnp.concatenate([pole_set[1:] - pole_set[:-1], jnp.ones((1,), jnp.float32)])
    fraction = jax.random.uniform(seeded_generators[1], (P_SIZE,), jnp.float32, 0.15, 0.85)
    root_set = pole_set + fraction * spacing
    magnitude = jnp.exp(jax.random.uniform(seeded_generators[2], (P_SIZE,), jnp.float32, math.log(0.3), math.log(3.0)))
    sign_set = jnp.where(jax.random.uniform(seeded_generators[3], (P_SIZE,)) < 0.5, -1.0, 1.0)
    weight = sign_set * magnitude
    entries = weight[:, None] / (pole_set[:, None] - root_set[None, :])
    return entries / jnp.sqrt(jnp.sum(entries * entries, axis=0, keepdims=True))


def draw_refl_v(key, part):
    seeded_generators = jax.random.split(jax.random.fold_in(key, 11), 7)
    gaussian = jax.random.normal(seeded_generators[0], (PASS_TOTAL, PIECES_PER_PASS + 1, HALF_WIDTH, HALF_WIDTH), jnp.float32)
    orthogonal, _ = jnp.linalg.qr(gaussian)
    fast_share = 0.5
    tilt = 0.002
    fast_mode = jax.random.uniform(seeded_generators[1], (PASS_TOTAL, 1, HALF_WIDTH)) < fast_share
    slow_loss = jax.random.uniform(seeded_generators[2], (PASS_TOTAL, 1, HALF_WIDTH), jnp.float32, 0.2, 0.5)
    gradual_preserve = 10.0 ** (-slow_loss / PIECES_PER_PASS)
    quick_location = jax.random.randint(seeded_generators[3], (PASS_TOTAL, 2), 0, PIECES_PER_PASS - 2)
    storage_locations = jnp.arange(PIECES_PER_PASS)
    quick_pairing = jnp.any(storage_locations[None, :, None] == quick_location[:, None, :], axis=2)
    quick_preserve = jax.random.uniform(seeded_generators[4], (PASS_TOTAL, PIECES_PER_PASS, HALF_WIDTH), jnp.float32, 0.7, 0.9)
    gradual_preserve = jnp.where(quick_pairing[:, :, None], gradual_preserve * quick_preserve, gradual_preserve)
    fast_keep = 1.0 - jnp.exp(jax.random.uniform(seeded_generators[5], (PASS_TOTAL, PIECES_PER_PASS, HALF_WIDTH), jnp.float32, math.log(0.02), math.log(0.1)))
    retained = jnp.where(fast_mode, fast_keep, gradual_preserve)
    mode_beta = (1.0 - jnp.sqrt(1.0 - retained * retained)) / retained
    upper_part = orthogonal[:, :PIECES_PER_PASS]
    lower_part = -orthogonal[:, 1:] * mode_beta[:, :, None, :]
    stacked = jnp.concatenate([upper_part, lower_part], axis=2)
    triangle_part = jax.random.uniform(seeded_generators[6], (PASS_TOTAL, PIECES_PER_PASS, HALF_WIDTH, HALF_WIDTH), jnp.float32, -tilt, tilt)
    mixing = jnp.triu(triangle_part, 1) + jnp.eye(HALF_WIDTH, dtype=jnp.float32)
    tilted = jnp.einsum('pgik,pgkj->pgij', stacked, mixing, precision=lax.Precision.HIGHEST)
    return jnp.clip(tilted, -1.0, 1.0)


def levels(own_key, extent, shards, smallest, largest):
    factor_of = 1.0
    for dim, parts in shards:
        steps = jax.random.uniform(jax.random.fold_in(jax.random.fold_in(own_key, 6), dim), (parts,), jnp.float32, smallest / len(shards), largest / len(shards))
        factor_of = factor_of * jnp.repeat(jnp.exp(steps), extent[dim] // parts).reshape((-1,) + (1,) * (len(extent) - 1 - dim))
    return factor_of


def scatter_about(own_key, dims, width, most, pieces=(), held_as=jnp.bfloat16):
    factor_of = levels(own_key, dims, pieces, -0.22, 0.18) if pieces else 1.0
    drawn = jax.random.normal(own_key, dims, jnp.float32) * width * factor_of
    return jnp.minimum(jnp.maximum(drawn, -most), most).astype(held_as)


def setup_inputs(seed: int = 0) -> dict:
    key_of = jax.random.split(jax.random.key(seed), 5)
    panel = scatter_about(key_of[0], (P_SIZE, N), 1.0, 6.0, ((0, 4), (1, 8)), jnp.float32)
    cauchy = draw_cauchy(jax.random.fold_in(key_of[4], 71), 0)
    refl_v = draw_refl_v(jax.random.fold_in(key_of[4], 71), 0)
    block_start = jax.random.randint(key_of[3], (PASS_TOTAL,), 0, HALF_WIDTH).astype(jnp.int32)
    return dict(panel=panel, cauchy=cauchy, refl_v=refl_v, block_start=block_start)


HIGHEST = lax.Precision.HIGHEST

def upper_inverse(gram_matrix):
    identity = jnp.eye(HALF_WIDTH, dtype=jnp.float32)
    halves = 0.5 * jnp.sum(gram_matrix * identity, axis=1)
    nilpotent = jnp.triu(gram_matrix, 1) / halves[:, None]
    power = nilpotent
    result = identity - nilpotent
    reach = 2
    while reach < HALF_WIDTH:
        power = jnp.dot(power.astype(jnp.float32), power.astype(jnp.float32), precision=HIGHEST, preferred_element_type=jnp.float32)
        result = jnp.dot(result.astype(jnp.float32), (identity + power).astype(jnp.float32), precision=HIGHEST, preferred_element_type=jnp.float32)
        reach = reach * 2
    return result / halves[None, :]

def reflector(vblock):
    gram_matrix = jnp.dot(vblock.T.astype(jnp.float32), vblock.astype(jnp.float32), precision=HIGHEST, preferred_element_type=jnp.float32)
    triangle = upper_inverse(gram_matrix)
    return jnp.dot(vblock.astype(jnp.float32), triangle.T.astype(jnp.float32), precision=HIGHEST, preferred_element_type=jnp.float32)

def apply_sweep(current, reflectors, anchor):
    anchor = anchor.astype(jnp.int32)
    segment = lax.dynamic_slice_in_dim(current, anchor, N - HALF_WIDTH, 1)
    segments = segment.reshape(P_SIZE, PIECES_PER_PASS - 1, HALF_WIDTH).transpose(1, 0, 2)

    def advance(moving, inputs):
        vblock, fresh_seg = inputs
        stacked = jnp.concatenate([moving, fresh_seg], axis=1)
        scaled_v = reflector(vblock)
        inner = jnp.dot(stacked.astype(jnp.float32), scaled_v.astype(jnp.float32), precision=HIGHEST, preferred_element_type=jnp.float32)
        mixed_rows = stacked - jnp.dot(inner.astype(jnp.float32), vblock.T.astype(jnp.float32), precision=HIGHEST, preferred_element_type=jnp.float32)
        return (mixed_rows[:, HALF_WIDTH:], mixed_rows[:, :HALF_WIDTH])
    last_carry, outputs = lax.scan(advance, segments[0], (reflectors[:PIECES_PER_PASS - 2], segments[1:]))
    finished = jnp.concatenate([outputs, last_carry[None]], axis=0)
    updated = finished.transpose(1, 0, 2).reshape(P_SIZE, N - HALF_WIDTH)
    return lax.dynamic_update_slice_in_dim(current, updated, anchor, 1)

def reference(panel, cauchy, refl_v, block_start):
    current = jnp.dot(cauchy.T.astype(jnp.float32), panel.astype(jnp.float32), precision=HIGHEST, preferred_element_type=jnp.float32)
    for sweep_turn in range(PASS_TOTAL):
        current = apply_sweep(current, refl_v[sweep_turn], block_start[sweep_turn])
    return current
```

```python
import functools

import jax
import jax.numpy as jnp
from jax import lax
from jax.experimental import pallas as pl
from jax.experimental.pallas import tpu as pltpu
from jax.sharding import PartitionSpec as P

F32, BF16 = jnp.float32, jnp.bfloat16
VMEM = pl.BlockSpec(memory_space=pltpu.VMEM)
SMEM = pl.BlockSpec(memory_space=pltpu.SMEM)
NN = (((1,), (0,)), ((), ()))
NT = (((1,), (1,)), ((), ()))
TN = (((0,), (0,)), ((), ()))


def split(value):
    high = value.astype(BF16)
    return high, (value - high.astype(F32)).astype(BF16)


def dot(left, right, dims=NN):
    return lax.dot_general(left, right, dims, preferred_element_type=F32)


def wide(value):
    return jnp.concatenate(split(value), axis=1)


def apply(left, high, low):
    left_high, left_low = split(left)
    return dot(
        jnp.concatenate([left_high, left_low, left_high], axis=1),
        jnp.concatenate([high, high, low], axis=0),
    )


def times(left, right):
    return apply(left, *split(right))


def eye(rows, columns):
    shape = (rows, columns)
    return lax.broadcasted_iota(jnp.int32, shape, 0) == lax.broadcasted_iota(jnp.int32, shape, 1)


def upper_inverses(grams):
    spread = grams[0].shape[0]
    diagonal = eye(spread, spread)
    identity = diagonal.astype(F32)
    above = lax.broadcasted_iota(jnp.int32, (spread, spread), 0) < lax.broadcasted_iota(
        jnp.int32, (spread, spread), 1
    )
    halves = [jnp.where(diagonal, 0.5 * gram, 0.0) for gram in grams]
    columns = [jnp.sum(half, axis=0, keepdims=True) for half in halves]
    powers = [
        jnp.where(above, gram, 0.0) / jnp.sum(half, axis=1, keepdims=True)
        for gram, half in zip(grams, halves)
    ]
    results = [identity - power for power in powers]
    pairs = [wide(power) for power in powers]
    products = [dot(pair, jnp.concatenate([pair, pair], axis=0)) for pair in pairs]
    powers = [product[:, :spread] + product[:, spread:] for product in products]
    reach = 2
    while reach < spread:
        reach *= 2
        pairs = [wide(power) for power in powers]
        lefts = [wide(result) for result in results]
        if reach < spread:
            lefts = [jnp.concatenate([left, pair], axis=0) for left, pair in zip(lefts, pairs)]
        products = [
            dot(left, jnp.concatenate([pair, pair], axis=0)) for left, pair in zip(lefts, pairs)
        ]
        products = [product[:, :spread] + product[:, spread:] for product in products]
        results = [result + product[:spread] for result, product in zip(results, products)]
        if reach < spread:
            powers = [product[spread:] for product in products]
    return [result / column for result, column in zip(results, columns)]


def reflect_kernel(run, last, limit, v, *refs):
    if last:
        before, refs = refs[0], refs[1:]
        k_high, k_low, q_high, q_low, maps, reach, total, seam = refs
    else:
        k_high, k_low, q_high, q_low, maps, seam = refs
    blocks, double, spread = v.shape
    pairs = [wide(v[b]) for b in range(blocks)]
    grams = [dot(pair, pair, TN) for pair in pairs]
    grams = [
        (g[:spread, :spread] + g[spread:, spread:]) + (g[:spread, spread:] + g[spread:, :spread])
        for g in grams
    ]
    triangles = upper_inverses(grams)
    unit = eye(double, double).astype(F32)
    scaled = []
    for b in range(blocks):
        high, low = split(triangles[b])
        right = jnp.concatenate(
            [jnp.concatenate([high, high], axis=1), jnp.concatenate([low, low], axis=1)], axis=0
        )
        product = dot(pairs[b], right, NT)
        scaled.append(product[:, :spread] + product[:, spread:])
    for b in range(blocks):
        high, low = split(scaled[b])
        v_high, v_low = pairs[b][:, :spread], pairs[b][:, spread:]
        product = dot(
            jnp.concatenate([high, low, high], axis=1),
            jnp.concatenate([v_high, v_high, v_low], axis=1),
            NT,
        )
        high, low = split(unit - jnp.where(b <= limit[0], product, 0.0))
        k_high[b // run, b % run] = high
        k_low[b // run, b % run] = low
    runs = blocks // run
    state = [None] * runs
    for step in range(run):
        for j in range(runs):
            high, low = k_high[j, step, :spread, :], k_low[j, step, :spread, :]
            if step == 0:
                both = high.astype(F32) + low.astype(F32)
            else:
                both = apply(state[j], high, low)
            state[j] = both[:, spread:]
            out = both[:, :spread]
            high, low = split(out)
            q_high[j, :, step * spread : (step + 1) * spread] = high
            q_low[j, :, step * spread : (step + 1) * spread] = low
            if not last and j == 0 and step < 2:
                seam[:, step * spread : (step + 1) * spread] = out
    for j in range(runs):
        maps[j] = state[j]
    if last:
        every = [before[j] for j in range(before.shape[0])] + state
        so_far = every[0]
        for j in range(1, len(every)):
            reach[j - 1] = so_far
            if j == len(every) - 1:
                seam[...] = times(so_far, out)
            so_far = times(so_far, every[j])
        total[...] = so_far


def reflect(refl_v, sweep, part, parts, run, before=None):
    count = refl_v.shape[1] // parts
    double, spread = refl_v.shape[2:]
    runs = count // run
    last = before is not None
    slot_first = lax.axis_index("row") * refl_v.shape[1]
    slot_total = lax.axis_size("row") * refl_v.shape[1]
    limit = (slot_total - 3 - slot_first - part * count).astype(jnp.int32).reshape(1)
    kept = jax.ShapeDtypeStruct((runs, run, double, double), BF16)
    response = jax.ShapeDtypeStruct((runs, spread, run * spread), BF16)
    maps = jax.ShapeDtypeStruct((runs, spread, spread), F32)
    shapes = [kept, kept, response, response, maps]
    if last:
        shapes += [
            jax.ShapeDtypeStruct((parts * runs - 1, spread, spread), F32),
            jax.ShapeDtypeStruct((spread, spread), F32),
            jax.ShapeDtypeStruct((spread, spread), F32),
        ]
    else:
        shapes += [jax.ShapeDtypeStruct((spread, 2 * spread), F32)]
    block = pl.BlockSpec((None, count, double, spread), lambda i: (sweep, part, 0, 0))

    def whole(shape):
        rank = len(shape.shape)
        return pl.BlockSpec(shape.shape, lambda i: (0,) * rank)

    inputs, specs = [limit, refl_v], [SMEM, block]
    if last:
        inputs.append(before)
        specs.append(whole(before))
    return pl.pallas_call(
        functools.partial(reflect_kernel, run, last),
        grid=(1,),
        out_shape=shapes,
        in_specs=specs,
        out_specs=[whole(shape) for shape in shapes],
        compiler_params=pltpu.CompilerParams(vmem_limit_bytes=32 << 20),
        cost_estimate=pl.CostEstimate(
            flops=count * 600_000_000, bytes_accessed=count * 400_000, transcendentals=0
        ),
    )(*inputs)


def merge_kernel(place, cauchy, *refs):
    count = len(refs) // 2
    pieces, outs = refs[:count], refs[count:]
    rows, width = pieces[0].shape
    mine = place[0]
    left, right = [], []
    for k in range(count):
        owner = lax.rem(mine - k + count, count)
        block = cauchy[pl.ds(pl.multiple_of(owner * rows, rows), rows), :]
        left.append(block)
        right.append(pieces[k][...])
    left_high, left_low = split(jnp.concatenate(left, axis=0))
    right_high, right_low = split(jnp.concatenate(right, axis=0))
    merged = dot(left_high, right_high, TN)
    merged = merged + (dot(left_high, right_low, TN) + dot(left_low, right_high, TN))
    for k in range(count):
        owner = lax.rem(mine + k, count)
        for other in range(count):

            @pl.when(owner == other)
            def _():
                outs[k][...] = merged[other * rows : (other + 1) * rows, :]


def shifted(array, axis, by, around=False):
    devices = lax.axis_size(axis)
    if around:
        pairs = [(i, (i + by) % devices) for i in range(devices)]
    else:
        pairs = [(i, i + by) for i in range(devices) if 0 <= i + by < devices]
    return lax.ppermute(array, axis, pairs)


def merge(panel, cauchy):
    rows, columns = panel.shape
    count = lax.axis_size("col")
    mine = lax.axis_index("col")
    width = columns // count
    pieces = [
        lax.dynamic_slice_in_dim(panel, lax.rem(mine + k, count) * width, width, 1)
        for k in range(count)
    ]
    pieces = [pieces[0]] + [shifted(pieces[k], "col", k, True) for k in range(1, count)]
    shape = jax.ShapeDtypeStruct((rows, width), F32)
    outs = pl.pallas_call(
        merge_kernel,
        out_shape=[shape] * count,
        in_specs=[SMEM] + [VMEM] * (1 + count),
        out_specs=[VMEM] * count,
        compiler_params=pltpu.CompilerParams(vmem_limit_bytes=16 << 20),
        cost_estimate=pl.CostEstimate(
            flops=1_000_000_000, bytes_accessed=2_000_000, transcendentals=0
        ),
    )(mine.astype(jnp.int32).reshape(1), cauchy, *pieces)
    return [outs[0]] + [shifted(outs[k], "col", k, True) for k in range(1, count)]


def rolled(value, left):
    width = value.shape[1]
    return pltpu.roll(value, lax.rem(width - left, width), 1)


def chain_step(step, run, k_high, k_low, segments, carry, y_local):
    spread = carry.shape[2]
    for j in range(carry.shape[0]):
        slot = j * run + step
        both = apply(
            jnp.concatenate([carry[j], segments[slot + 1]], axis=1), k_high[j], k_low[j]
        )
        y_local[slot] = both[:, :spread]
        carry[j] = both[:, spread:]


def chain_start(first, aligned, segments, carry):
    spread = carry.shape[2]
    for slot in range(segments.shape[0]):
        segments[slot] = aligned[:, slot * spread : (slot + 1) * spread]
    carry[...] = jnp.zeros_like(carry)

    @pl.when(first)
    def _():
        carry[0] = segments[0]


def chain_end(maps, carry, joins, state):
    runs = carry.shape[0]
    so_far = carry[0]
    joins[0] = jnp.zeros_like(so_far)
    for j in range(1, runs):
        joins[j] = so_far
        so_far = times(so_far, maps[j]) + carry[j]
    state[...] = so_far


def first_kernel(count, run, place, start, k_high, k_low, maps, after, *refs):
    pieces, (y_local, joins, state, head, home, segments, carry) = refs[:count], refs[count:]
    step = pl.program_id(0)
    spread = carry.shape[2]
    rows, width = pieces[0].shape
    columns = home.shape[1]

    @pl.when(step == 0)
    def _():
        for k in range(count):
            owner = lax.rem(place[1] - k + count, count)
            home[:, pl.ds(pl.multiple_of(owner * width, width), width)] = pieces[k][...]
        offset = start[0]
        head[...] = pltpu.roll(home[:, :spread], lax.rem(spread - offset, spread), 1)
        aligned = rolled(jnp.concatenate([home[...], after[...]], axis=1), offset)
        chain_start(place[0] == 0, aligned[:, : columns + spread], segments, carry)

    chain_step(step, run, k_high, k_low, segments, carry, y_local)

    @pl.when(step == run - 1)
    def _():
        chain_end(maps, carry, joins, state)


def entering(states, totals):
    so_far, earlier = states[-1][...], jnp.zeros_like(states[-1][...])
    for k in range(len(totals) - 1, -1, -1):
        earlier = so_far
        so_far = times(so_far, totals[k][...]) + states[k][...]
    return earlier, so_far


def settled(incoming, reach, joins, q_high, q_low, y_local, place):
    runs = joins.shape[0]
    spread = incoming.shape[1]
    run = q_high.shape[2] // spread
    for j in range(runs):
        enters = incoming if j == 0 else joins[j] + times(incoming, reach[j - 1])
        added = apply(enters, q_high[j], q_low[j])
        for step in range(run):
            slot = j * run + step
            place(slot, y_local[slot] + added[:, step * spread : (step + 1) * spread])


def second_kernel(shifts, run, place, start, k_high, k_low, maps, *refs):
    states, refs = refs[:shifts], refs[shifts:]
    totals, refs = refs[: shifts - 1], refs[shifts - 1 :]
    (
        q_high,
        q_low,
        reach,
        joins_in,
        y_in,
        state_in,
        total_in,
        head,
        y_after,
        seam_after,
        q_last,
        y_local,
        joins,
        state,
        head_out,
        tail,
        line,
        segments,
        carry,
    ) = refs
    step = pl.program_id(0)
    spread = carry.shape[2]
    slots = y_in.shape[0]

    @pl.when(step == 0)
    def _():
        incoming = entering(states, totals)[1]

        def put(slot, value):
            line[:, (slot + 1) * spread : (slot + 2) * spread] = value

        line[:, :spread] = head[...]
        settled(incoming, reach, joins_in, q_high, q_low, y_in, put)
        leaving = times(incoming, total_in[...]) + state_in[...]
        added = times(leaving, seam_after[...])
        for extra in range(2):
            put(slots + extra, y_after[extra] + added[:, extra * spread : (extra + 1) * spread])
        shift = start[1] + spread - start[0]
        head_out[...] = pltpu.roll(
            line[:, : 2 * spread],
            lax.rem(4 * spread - (shift - spread), 2 * spread),
            1,
        )[:, :spread]
        aligned = rolled(line[...], shift)
        chain_start(place[0] == 0, aligned[:, : (slots + 1) * spread], segments, carry)

    chain_step(step, run, k_high, k_low, segments, carry, y_local)

    @pl.when(step == run - 1)
    def _():
        chain_end(maps, carry, joins, state)
        tail[...] = y_local[slots - 1] + times(joins[joins.shape[0] - 1], q_last[...])


def final_kernel(shifts, place, start, *refs):
    states, refs = refs[:shifts], refs[shifts:]
    totals, refs = refs[: shifts - 1], refs[shifts - 1 :]
    q_high, q_low, reach, joins, y_local, head, tail, seam, out, line = refs
    spread = head.shape[1]
    earlier, incoming = entering(states, totals)

    def put(slot, value):
        line[:, (slot + 1) * spread : (slot + 2) * spread] = value

    line[:, :spread] = jnp.where(
        place[0] == 0, head[...], tail[...] + times(earlier, seam[...])
    )
    settled(incoming, reach, joins, q_high, q_low, y_local, put)
    out[...] = rolled(line[...], spread - start[1])[:, : out.shape[1]]


def per_step(array):
    runs, _, double, _ = array.shape
    return pl.BlockSpec((runs, None, double, double), lambda step: (0, step, 0, 0))


def fixed(array):
    rank = len(array.shape)
    return pl.BlockSpec(array.shape, lambda step: (0,) * rank)


def joined(first, second):
    return jnp.concatenate([first, second], axis=0)


def shards(panel, cauchy, refl_v, block_start):
    rows, columns = panel.shape
    spread = refl_v.shape[3]
    slots = refl_v.shape[1]
    run = 4
    runs = slots // run
    devices, count = lax.axis_size("row"), lax.axis_size("col")
    place = jnp.stack([lax.axis_index("row"), lax.axis_index("col")]).astype(jnp.int32)

    pieces = merge(panel, cauchy)
    k00 = reflect(refl_v, 0, 0, 2, run)
    k01 = reflect(refl_v, 0, 1, 2, run, k00[4])
    k10 = reflect(refl_v, 1, 0, 2, run)
    k11 = reflect(refl_v, 1, 1, 2, run, k10[4])

    mine = place[1]
    opening = pieces[0][:, : 2 * spread]
    for k in range(1, count):
        opening = jnp.where(mine == k, pieces[k][:, : 2 * spread], opening)
    after = shifted(opening, "row", -1)

    high1, low1, qh1, ql1, maps1 = (joined(a, b) for a, b in zip(k00[:5], k01[:5]))
    reach1, total1 = k01[5], k01[6]
    high2, low2, qh2, ql2, maps2 = (joined(a, b) for a, b in zip(k10[:5], k11[:5]))
    reach2, total2, seam2 = k11[5], k11[6], k11[7]

    y_shape = jax.ShapeDtypeStruct((slots, rows, spread), F32)
    joins_shape = jax.ShapeDtypeStruct((runs, rows, spread), F32)
    state_shape = jax.ShapeDtypeStruct((rows, spread), F32)
    scratch = [
        pltpu.VMEM((slots + 1, rows, spread), F32),
        pltpu.VMEM((runs, rows, spread), F32),
    ]
    shapes = [y_shape, joins_shape, state_shape, state_shape]
    y1, joins1, state1, head1 = pl.pallas_call(
        functools.partial(first_kernel, count, run),
        grid=(run,),
        out_shape=shapes,
        in_specs=[SMEM, SMEM, per_step(high1), per_step(low1), fixed(maps1), fixed(after)]
        + [fixed(piece) for piece in pieces],
        out_specs=[fixed(shape) for shape in shapes],
        scratch_shapes=[pltpu.VMEM((rows, columns), F32)] + scratch,
        compiler_params=pltpu.CompilerParams(vmem_limit_bytes=32 << 20),
        cost_estimate=pl.CostEstimate(
            flops=3_000_000_000, bytes_accessed=8_000_000, transcendentals=0
        ),
    )(place, block_start, high1, low1, maps1, after, *pieces)

    totals1 = [shifted(total1, "row", k) for k in range(1, devices - 1)]
    states1 = [shifted(state1, "row", k) for k in range(1, devices)]
    seam_after = shifted(k00[5], "row", -1)
    y_after = shifted(y1[:2], "row", -1)

    totals2 = [shifted(total2, "row", k) for k in range(1, devices - 1)]
    seam_before = shifted(seam2, "row", 1)
    q_last = qh2[-1][:, -spread:].astype(F32) + ql2[-1][:, -spread:].astype(F32)
    inputs = (
        [maps2]
        + states1
        + totals1
        + [qh1, ql1, reach1, joins1, y1, state1, total1, head1, y_after, seam_after, q_last]
    )
    shapes = [y_shape, joins_shape, state_shape, state_shape, state_shape]
    y2, joins2, state2, head2, tail2 = pl.pallas_call(
        functools.partial(second_kernel, devices - 1, run),
        grid=(run,),
        out_shape=shapes,
        in_specs=[SMEM, SMEM, per_step(high2), per_step(low2)] + [fixed(a) for a in inputs],
        out_specs=[fixed(shape) for shape in shapes],
        scratch_shapes=[pltpu.VMEM((rows, columns + 3 * spread), F32)] + scratch,
        compiler_params=pltpu.CompilerParams(vmem_limit_bytes=32 << 20),
        cost_estimate=pl.CostEstimate(
            flops=4_000_000_000, bytes_accessed=8_000_000, transcendentals=0
        ),
    )(place, block_start, high2, low2, *inputs)

    states2 = [shifted(state2, "row", k) for k in range(1, devices)]
    tail_before = shifted(tail2, "row", 1)
    inputs = states2 + totals2 + [qh2, ql2, reach2, joins2, y2, head2, tail_before, seam_before]
    return pl.pallas_call(
        functools.partial(final_kernel, devices - 1),
        out_shape=jax.ShapeDtypeStruct((rows, columns), F32),
        in_specs=[SMEM, SMEM] + [VMEM] * len(inputs),
        out_specs=VMEM,
        scratch_shapes=[pltpu.VMEM((rows, columns + spread), F32)],
        compiler_params=pltpu.CompilerParams(vmem_limit_bytes=32 << 20),
        cost_estimate=pl.CostEstimate(
            flops=1_000_000_000, bytes_accessed=4_000_000, transcendentals=0
        ),
    )(place, block_start, *inputs)


def solution(mesh):
    placed = (P("col", "row"), P(), P(None, "row", None, None), P())
    return jax.shard_map(
        shards, mesh=mesh, in_specs=placed, out_specs=P("col", "row"), check_vma=False
    )
```

```python
import functools

import jax
import jax.numpy as jnp
from jax import lax
from jax.experimental import pallas as pl
from jax.experimental.pallas import tpu as pltpu
from jax.sharding import PartitionSpec as P

F32, BF16 = jnp.float32, jnp.bfloat16
VMEM = pl.BlockSpec(memory_space=pltpu.VMEM)
SMEM = pl.BlockSpec(memory_space=pltpu.SMEM)
NN = (((1,), (0,)), ((), ()))
NT = (((1,), (1,)), ((), ()))
TN = (((0,), (0,)), ((), ()))


def split(value):
    high = value.astype(BF16)
    return high, (value - high.astype(F32)).astype(BF16)


def dot(left, right, dims=NN):
    return lax.dot_general(left, right, dims, preferred_element_type=F32)


def wide(value):
    return jnp.concatenate(split(value), axis=1)


def tall(value):
    terms = [jnp.concatenate([term, term], axis=1) for term in split(value)]
    return jnp.concatenate(terms, axis=0)


def doubled(rows_high, rows_low):
    return jnp.concatenate([rows_high, rows_low], axis=0)


def folded(product):
    half = product.shape[0] // 2
    return product[:half] + product[half:]


def apply(left, high, low):
    if left.shape[1] <= 128:
        return folded(dot(tall(left), doubled(high, low)))
    left_high, left_low = split(left)
    return folded(dot(jnp.concatenate([left_high, left_low], axis=0), high)) + dot(left_high, low)


def times(left, right):
    return apply(left, *split(right))


def eye(rows, columns):
    shape = (rows, columns)
    return lax.broadcasted_iota(jnp.int32, shape, 0) == lax.broadcasted_iota(jnp.int32, shape, 1)


def upper_inverses(grams):
    spread = grams[0].shape[0]
    base = spread // 4
    diagonal = eye(spread, spread)
    above = lax.broadcasted_iota(jnp.int32, (spread, spread), 0) < lax.broadcasted_iota(
        jnp.int32, (spread, spread), 1
    )
    halves = [jnp.where(diagonal, 0.5 * gram, 0.0) for gram in grams]
    columns = [jnp.sum(half, axis=0, keepdims=True) for half in halves]
    scaled = [
        jnp.where(above, gram, 0.0) / jnp.sum(half, axis=1, keepdims=True)
        for gram, half in zip(grams, halves)
    ]

    def owner(size):
        return lax.broadcasted_iota(jnp.int32, (size, spread), 1) // size

    def compact(value, size, row=lambda block: block):
        owns = owner(size)
        result = value[row(0) * size : (row(0) + 1) * size]
        for block in range(1, spread // size):
            at = row(block) * size
            result = jnp.where(owns == block, value[at : at + size], result)
        return result

    def expanded(value, size, row=lambda block: block):
        owns = owner(size)
        masks = [(owns == block).astype(BF16) for block in range(spread // size)]
        terms = []
        for term in split(value):
            rows = [jnp.zeros_like(term)] * (spread // size)
            for block, mask in enumerate(masks):
                if row(block) is not None:
                    rows[row(block)] = term * mask
            terms.append(jnp.concatenate(rows, axis=0))
        return doubled(*terms)

    size = base
    unit = compact(diagonal.astype(F32), size)
    powers = [compact(value, size) for value in scaled]
    results = [unit - power for power in powers]
    rights = [expanded(power, size) for power in powers]
    powers = [folded(dot(tall(power), right)) for power, right in zip(powers, rights)]
    reach = 2
    while reach < size:
        reach *= 2
        rights = [expanded(power, size) for power in powers]
        if reach < size:
            lefts = [jnp.concatenate([r, p], axis=0) for r, p in zip(results, powers)]
        else:
            lefts = results
        products = [folded(dot(tall(left), right)) for left, right in zip(lefts, rights)]
        results = [result + product[:size] for result, product in zip(results, products)]
        if reach < size:
            powers = [product[size:] for product in products]
    while size < spread:
        odd = lax.rem(owner(size), 2) == 1
        edges = [
            jnp.where(odd, compact(value, size, lambda block: block & ~1), 0.0) for value in scaled
        ]
        rights = [expanded(result, size) for result in results]
        products = [folded(dot(tall(edge), right)) for edge, right in zip(edges, rights)]
        rights = [
            expanded(product, size, lambda block: block - 1 if block & 1 else None)
            for product in products
        ]
        products = [folded(dot(tall(result), right)) for result, right in zip(results, rights)]
        results = [
            jnp.concatenate(
                [jnp.where(odd, -product, result), jnp.where(odd, result, 0.0)], axis=0
            )
            for result, product in zip(results, products)
        ]
        size *= 2
    return [result / column for result, column in zip(results, columns)]


def reflect_kernel(
    run, sweep, last_slot, place, source,
    k_high, k_low, q_high, q_low, maps, reach, total, first, last, final,
):
    blocks, double, spread = source.shape[1:]
    limit = last_slot - place[0] * blocks
    pairs = [wide(source[sweep, b]) for b in range(blocks)]
    grams = [dot(pair, pair, TN) for pair in pairs]
    grams = [
        (g[:spread, :spread] + g[spread:, spread:]) + (g[:spread, spread:] + g[spread:, :spread])
        for g in grams
    ]
    triangles = upper_inverses(grams)
    unit = eye(double, double).astype(F32)
    scaled = []
    for b in range(blocks):
        high, low = split(triangles[b])
        right = jnp.concatenate(
            [jnp.concatenate([high, high], axis=1), jnp.concatenate([low, low], axis=1)], axis=0
        )
        product = dot(pairs[b], right, NT)
        scaled.append(product[:, :spread] + product[:, spread:])
    for b in range(blocks):
        product = folded(dot(tall(scaled[b]), pairs[b], NT))
        high, low = split(unit - jnp.where(b <= limit, product, 0.0))
        k_high[b] = high
        k_low[b] = low
    runs = blocks // run
    state, out = [None] * runs, [None] * runs
    for step in range(run):
        for j in range(runs):
            b = j * run + step
            high, low = k_high[b, :spread, :], k_low[b, :spread, :]
            if step == 0:
                both = high.astype(F32) + low.astype(F32)
            else:
                both = apply(state[j], high, low)
            state[j] = both[:, spread:]
            out[j] = both[:, :spread]
            high, low = split(out[j])
            q_high[j, :, step * spread : (step + 1) * spread] = high
            q_low[j, :, step * spread : (step + 1) * spread] = low
            if j == 0 and step < 2:
                first[:, step * spread : (step + 1) * spread] = out[j]
    so_far = state[0]
    for j in range(runs):
        maps[j] = state[j]
        if j:
            reach[j - 1] = so_far
            if j == runs - 1:
                last[...] = out[j]
                final[...] = times(so_far, out[j])
            so_far = times(so_far, state[j])
    total[...] = so_far


def reflect(place, refl_v, sweep, run):
    count, double, spread = refl_v.shape[1:]
    runs = count // run
    last_slot = lax.axis_size("row") * count - 3
    square = jax.ShapeDtypeStruct((spread, spread), F32)
    shapes = [
        jax.ShapeDtypeStruct((count, double, double), BF16),
        jax.ShapeDtypeStruct((count, double, double), BF16),
        jax.ShapeDtypeStruct((runs, spread, run * spread), BF16),
        jax.ShapeDtypeStruct((runs, spread, run * spread), BF16),
        jax.ShapeDtypeStruct((runs, spread, spread), F32),
        jax.ShapeDtypeStruct((runs - 1, spread, spread), F32),
        square,
        jax.ShapeDtypeStruct((spread, 2 * spread), F32),
        square,
        square,
    ]
    return pl.pallas_call(
        functools.partial(reflect_kernel, run, sweep, last_slot),
        out_shape=shapes,
        in_specs=[SMEM, VMEM],
        out_specs=[VMEM] * len(shapes),
        compiler_params=pltpu.CompilerParams(vmem_limit_bytes=16 << 20),
        cost_estimate=pl.CostEstimate(
            flops=count * 500_000_000, bytes_accessed=count * 400_000, transcendentals=0
        ),
    )(place, refl_v)


def merge_kernel(owners, place, cauchy, *refs):
    pieces, (merged, chosen) = refs[:-2], refs[-2:]
    rows, columns = pieces[0].shape
    mine = place[1]
    chosen[...] = rolled(cauchy[...], mine * rows)[:, : chosen.shape[1]]
    left = [
        chosen[pl.ds(pl.multiple_of((mine ^ owner) * rows, rows), rows), :rows] for owner in owners
    ]
    left_high, left_low = split(jnp.concatenate(left, axis=0))
    step = columns // 4
    for part in range(4):
        at = slice(part * step, (part + 1) * step)
        right_high, right_low = split(jnp.concatenate([piece[:, at] for piece in pieces], axis=0))
        merged[:, at] = dot(left_high, right_high, TN) + (
            dot(left_high, right_low, TN) + dot(left_low, right_high, TN)
        )


def shifted(array, by):
    devices = lax.axis_size("row")
    return lax.ppermute(array, "row", [(i, (i + by) % devices) for i in range(devices)])


def swapped(array, axis, distance):
    devices = lax.axis_size(axis)
    return lax.ppermute(array, axis, [(i, i ^ distance) for i in range(devices)])


def merge(place, panel, cauchy, ready):
    rows, columns = panel.shape
    count = lax.axis_size("col")
    pieces, owners = [panel], [0]
    distance = count // 2
    while distance:
        pieces += [swapped(piece, "col", distance) for piece in pieces]
        if owners == [0]:
            pieces[-1] = lax.optimization_barrier((pieces[-1], ready))[0]
        owners += [owner ^ distance for owner in owners]
        distance //= 2
    return whole_call(
        functools.partial(merge_kernel, owners), jax.ShapeDtypeStruct((rows, columns), F32),
        1_000_000_000, [place], [cauchy] + pieces,
        [pltpu.VMEM((cauchy.shape[0], 128 * pl.cdiv(rows, 128)), F32)],
    )


def rolled(value, left):
    width = value.shape[1]
    return pltpu.roll(value, lax.rem(width - left, width), 1)


def chain(first, aligned, k_high, k_low, maps, y_local, joins, state):
    slots, rows, spread = y_local.shape
    runs = maps.shape[0]
    run = slots // runs

    def segment(slot):
        return aligned[:, slot * spread : (slot + 1) * spread]

    carry = [jnp.zeros((rows, spread), F32)] * runs
    carry[0] = jnp.where(first, segment(0), 0.0)
    for step in range(run):
        for j in range(runs):
            slot = j * run + step
            fresh = jnp.concatenate([carry[j], segment(slot + 1)], axis=1)
            both = apply(fresh, k_high[slot], k_low[slot])
            y_local[slot] = both[:, :spread]
            carry[j] = both[:, spread:]
    so_far = carry[0]
    joins[0] = jnp.zeros_like(so_far)
    for j in range(1, runs):
        joins[j] = so_far
        so_far = times(so_far, maps[j]) + carry[j]
    state[...] = so_far


def first_kernel(place, start, k_high, k_low, maps, home, after, y_local, joins, state, head):
    slots, rows, spread = y_local.shape
    offset = start[0]
    head[...] = pltpu.roll(home[:, :spread], lax.rem(spread - offset, spread), 1)
    aligned = rolled(jnp.concatenate([home[...], after[: home.shape[0]]], axis=1), offset)
    chain(place[0] == 0, aligned, k_high, k_low, maps, y_local, joins, state)


def is_upper(place, level):
    return lax.rem(place[0] // (1 << level), 2) == 1


def join_maps_kernel(level, top, place, mine, other, *refs):
    upper = is_upper(place, level)
    if level:
        inner, refs = refs[0], refs[1:]
    if top:
        final, refs = refs[0], refs[1:]
    high, both, inside = refs[:3]
    low = jnp.where(upper, other[...], mine[...])
    high[...] = jnp.where(upper, mine[...], other[...])
    both[...] = times(low, high[...])
    if level:
        inside[...] = jnp.where(upper, times(low, inner[...]), inner[...])
    else:
        inside[...] = jnp.where(upper, low, eye(*low.shape).astype(F32))
    if top:
        refs[3][...] = jnp.where(
            is_upper(place, level + 1), times(inside[...], final[...]), 0.0
        )


def join_states_kernel(level, top, place, mine, other, high, *refs):
    upper = is_upper(place, level)
    if level:
        inner, before, refs = refs[0], refs[1], refs[2:]
    if top:
        tail, final, refs = refs[0], refs[1], refs[2:]
    low = jnp.where(upper, other[...], mine[...])
    refs[0][...] = times(low, high[...]) + jnp.where(upper, mine[...], other[...])
    if level:
        enters = before[...] + jnp.where(upper, times(low, inner[...]), 0.0)
    else:
        enters = jnp.where(upper, low, 0.0)
    refs[1][...] = enters
    if top:
        refs[2][...] = tail[...] + times(enters, final[...])


def join_maps(place, total, final=None):
    levels = lax.axis_size("row").bit_length() - 1
    square = jax.ShapeDtypeStruct(total.shape, F32)
    inside, found, seam = None, [], None
    for level in range(levels - 1):
        top = final is not None and level == levels - 2
        arrays = [total, swapped(total, "row", 1 << level)]
        arrays += ([inside] if level else []) + ([final] if top else [])
        high, total, inside, *seam = whole_call(
            functools.partial(join_maps_kernel, level, top), [square] * (4 if top else 3),
            100_000_000, [place], arrays,
        )
        found.append((high, inside))
    return found, seam


def join_states(place, state, maps, tail=None, final=None):
    levels = len(maps) + 1
    segment = jax.ShapeDtypeStruct(state.shape, F32)
    enters, moved = None, None
    for level in range(levels - 1):
        top = tail is not None and level == levels - 2
        arrays = [state, swapped(state, "row", 1 << level), maps[level][0]]
        arrays += [maps[level - 1][1], enters] if level else []
        arrays += [tail, final] if top else []
        state, enters, *moved = whole_call(
            functools.partial(join_states_kernel, level, top), [segment] * (3 if top else 2),
            50_000_000, [place], arrays,
        )
    return swapped(state, "row", 1 << (levels - 1)), enters, moved


def entering(levels, place, half, inner, before):
    enters = jnp.where(is_upper(place, levels - 1), half[...], 0.0)
    return enters, before[...] + times(enters, inner[...])


def settled(incoming, reach, joins, q_high, q_low, y_local, put):
    runs = joins.shape[0]
    spread = incoming.shape[1]
    run = q_high.shape[2] // spread
    for j in range(runs):
        enters = incoming if j == 0 else joins[j] + times(incoming, reach[j - 1])
        added = apply(enters, q_high[j], q_low[j])
        for step in range(run):
            slot = j * run + step
            put(slot, y_local[slot] + added[:, step * spread : (step + 1) * spread])


def second_kernel(
    levels, place, start, half, inner, before, k_high, k_low, maps, q_high, q_low, reach, joins_in,
    y_in, state_in, total_in, head, y_after, after, final,
    y_local, joins, state, head_out, tail, line,
):
    slots, rows, spread = y_local.shape
    incoming = entering(levels, place, half, inner, before)[1]

    def put(slot, value):
        line[:, (slot + 1) * spread : (slot + 2) * spread] = value

    line[:, :spread] = head[...]
    settled(incoming, reach, joins_in, q_high, q_low, y_in, put)
    leaving = times(incoming, total_in[...]) + state_in[...]
    added = times(leaving, after[rows:])
    for extra in range(2):
        put(slots + extra, y_after[extra] + added[:, extra * spread : (extra + 1) * spread])
    ahead = start[1] - start[0]
    head_out[...] = pltpu.roll(
        line[:, : 2 * spread], lax.rem(4 * spread - ahead, 2 * spread), 1
    )[:, :spread]
    chain(
        place[0] == 0, rolled(line[...], ahead + spread), k_high, k_low, maps, y_local, joins, state
    )
    tail[...] = y_local[slots - 1] + times(joins[joins.shape[0] - 1], final[...])


def final_kernel(
    levels, place, start, half, inner, before, q_high, q_low, reach, joins, y_local, head, tail,
    final, out, line,
):
    spread = head.shape[1]
    earlier, incoming = entering(levels, place, half, inner, before)

    def put(slot, value):
        line[:, (slot + 1) * spread : (slot + 2) * spread] = value

    line[:, :spread] = jnp.where(
        place[0] == 0, head[...], tail[...] + times(earlier, final[...])
    )
    settled(incoming, reach, joins, q_high, q_low, y_local, put)
    out[...] = rolled(line[...], spread - start[1])[:, : out.shape[1]]


def whole_call(kernel, shapes, flops, scalars, arrays, scratch=()):
    return pl.pallas_call(
        kernel,
        out_shape=shapes,
        in_specs=[SMEM] * len(scalars) + [VMEM] * len(arrays),
        out_specs=jax.tree.map(lambda shape: VMEM, shapes),
        scratch_shapes=list(scratch),
        compiler_params=pltpu.CompilerParams(vmem_limit_bytes=8 << 20),
        cost_estimate=pl.CostEstimate(
            flops=flops, bytes_accessed=4_000_000, transcendentals=0
        ),
    )(*scalars, *arrays)


def run_length(slots):
    return next(size for size in (4, 2, 1) if slots % size == 0 and slots // size > 1)


def shards(panel, cauchy, refl_v, block_start):
    rows, columns = panel.shape
    slots, _, spread = refl_v.shape[1:]
    run = run_length(slots)
    levels = lax.axis_size("row").bit_length() - 1
    place = jnp.stack([lax.axis_index("row"), lax.axis_index("col")]).astype(jnp.int32)
    scalars = [place, block_start]
    shape = functools.partial(jax.ShapeDtypeStruct, dtype=F32)
    segment = shape((rows, spread))
    chained = [shape((slots, rows, spread)), shape((slots // run, rows, spread)), segment]

    high1, low1, qh1, ql1, maps1, reach1, total1, first1, _, _ = reflect(place, refl_v, 0, run)
    groups1, _ = join_maps(place, total1)
    high2, low2, qh2, ql2, maps2, reach2, total2, _, last2, final2 = reflect(place, refl_v, 1, run)
    groups2, [seam2] = join_maps(place, total2, final2)
    seam2 = shifted(seam2, 1)

    merged = merge(place, panel, cauchy, total1)
    after = shifted(jnp.concatenate([merged[:, : 2 * spread], first1], axis=0), -1)
    y1, joins1, state1, head1 = whole_call(
        first_kernel, chained + [segment], 3_000_000_000, scalars,
        [high1, low1, maps1, merged, after],
    )
    y_after = shifted(y1[:2], -1)
    half1, enters1, _ = join_states(place, state1, groups1)
    y2, joins2, state2, head2, tail2 = whole_call(
        functools.partial(second_kernel, levels), chained + [segment, segment], 4_000_000_000,
        scalars,
        [half1, groups1[-1][1], enters1, high2, low2, maps2, qh1, ql1, reach1, joins1, y1, state1,
         total1, head1, y_after, after, last2],
        [pltpu.VMEM((rows, columns + 3 * spread), F32)],
    )
    half2, enters2, [tail2] = join_states(place, state2, groups2, tail2, final2)
    tail2 = shifted(tail2, 1)
    return whole_call(
        functools.partial(final_kernel, levels), shape((rows, columns)), 1_000_000_000, scalars,
        [half2, groups2[-1][1], enters2, qh2, ql2, reach2, joins2, y2, head2, tail2, seam2],
        [pltpu.VMEM((rows, columns + spread), F32)],
    )


def solution(mesh):
    placed = (P("col", "row"), P(), P(None, "row", None, None), P())
    return jax.shard_map(
        shards, mesh=mesh, in_specs=placed, out_specs=P("col", "row"), check_vma=False
    )
```

```python
import functools

import jax
import jax.numpy as jnp
from jax import lax
from jax.experimental import pallas as pl
from jax.experimental.pallas import tpu as pltpu
from jax.sharding import PartitionSpec as P

F32, BF16 = jnp.float32, jnp.bfloat16
VMEM = pl.BlockSpec(memory_space=pltpu.VMEM)
SMEM = pl.BlockSpec(memory_space=pltpu.SMEM)
NN = (((1,), (0,)), ((), ()))
NT = (((1,), (1,)), ((), ()))
TN = (((0,), (0,)), ((), ()))


def split(value):
    high = value.astype(BF16)
    return high, (value - high.astype(F32)).astype(BF16)


def dot(left, right, dims=NN):
    return lax.dot_general(left, right, dims, preferred_element_type=F32)


def wide(value):
    return jnp.concatenate(split(value), axis=1)


def tall(value):
    terms = [jnp.concatenate([term, term], axis=1) for term in split(value)]
    return jnp.concatenate(terms, axis=0)


def doubled(rows_high, rows_low):
    return jnp.concatenate([rows_high, rows_low], axis=0)


def folded(product):
    half = product.shape[0] // 2
    return product[:half] + product[half:]


def apply(left, high, low):
    if left.shape[1] <= 128:
        return folded(dot(tall(left), doubled(high, low)))
    left_high, left_low = split(left)
    return folded(dot(jnp.concatenate([left_high, left_low], axis=0), high)) + dot(left_high, low)


def times(left, right):
    return apply(left, *split(right))


def eye(rows, columns):
    shape = (rows, columns)
    return lax.broadcasted_iota(jnp.int32, shape, 0) == lax.broadcasted_iota(jnp.int32, shape, 1)


def upper_inverses(grams):
    spread = grams[0].shape[0]
    base = spread // 4
    diagonal = eye(spread, spread)
    above = lax.broadcasted_iota(jnp.int32, (spread, spread), 0) < lax.broadcasted_iota(
        jnp.int32, (spread, spread), 1
    )
    halves = [jnp.where(diagonal, 0.5 * gram, 0.0) for gram in grams]
    columns = [jnp.sum(half, axis=0, keepdims=True) for half in halves]
    scaled = [
        jnp.where(above, gram, 0.0) / jnp.sum(half, axis=1, keepdims=True)
        for gram, half in zip(grams, halves)
    ]

    def owner(size):
        return lax.broadcasted_iota(jnp.int32, (size, spread), 1) // size

    def compact(value, size, row=lambda block: block):
        owns = owner(size)
        result = value[row(0) * size : (row(0) + 1) * size]
        for block in range(1, spread // size):
            at = row(block) * size
            result = jnp.where(owns == block, value[at : at + size], result)
        return result

    def expanded(value, size, row=lambda block: block):
        owns = owner(size)
        masks = [(owns == block).astype(BF16) for block in range(spread // size)]
        terms = []
        for term in split(value):
            rows = [jnp.zeros_like(term)] * (spread // size)
            for block, mask in enumerate(masks):
                if row(block) is not None:
                    rows[row(block)] = term * mask
            terms.append(jnp.concatenate(rows, axis=0))
        return doubled(*terms)

    size = base
    unit = compact(diagonal.astype(F32), size)
    powers = [compact(value, size) for value in scaled]
    results = [unit - power for power in powers]
    rights = [expanded(power, size) for power in powers]
    powers = [folded(dot(tall(power), right)) for power, right in zip(powers, rights)]
    reach = 2
    while reach < size:
        reach *= 2
        rights = [expanded(power, size) for power in powers]
        if reach < size:
            lefts = [jnp.concatenate([r, p], axis=0) for r, p in zip(results, powers)]
        else:
            lefts = results
        products = [folded(dot(tall(left), right)) for left, right in zip(lefts, rights)]
        results = [result + product[:size] for result, product in zip(results, products)]
        if reach < size:
            powers = [product[size:] for product in products]
    while size < spread:
        odd = lax.rem(owner(size), 2) == 1
        edges = [
            jnp.where(odd, compact(value, size, lambda block: block & ~1), 0.0) for value in scaled
        ]
        rights = [expanded(result, size) for result in results]
        products = [folded(dot(tall(edge), right)) for edge, right in zip(edges, rights)]
        rights = [
            expanded(product, size, lambda block: block - 1 if block & 1 else None)
            for product in products
        ]
        products = [folded(dot(tall(result), right)) for result, right in zip(results, rights)]
        results = [
            jnp.concatenate(
                [jnp.where(odd, -product, result), jnp.where(odd, result, 0.0)], axis=0
            )
            for result, product in zip(results, products)
        ]
        size *= 2
    return [result / column for result, column in zip(results, columns)]


def reflect_kernel(run, sweep, part, parts, last_slot, source, *refs):
    earlier = refs[:part]
    k_high, k_low, q_high, q_low, maps = refs[part : part + 5]
    refs = list(refs[part + 5 :])
    first = refs.pop(0) if part == 0 else None
    blocks, double, spread = k_high.shape[0], *source.shape[2:]
    limit = last_slot - lax.axis_index("row") * source.shape[1] - part * blocks
    pairs = [wide(source[sweep, part * blocks + b]) for b in range(blocks)]
    grams = [dot(pair, pair, TN) for pair in pairs]
    grams = [
        (g[:spread, :spread] + g[spread:, spread:]) + (g[:spread, spread:] + g[spread:, :spread])
        for g in grams
    ]
    triangles = upper_inverses(grams)
    unit = eye(double, double).astype(F32)
    scaled = []
    for b in range(blocks):
        high, low = split(triangles[b])
        right = jnp.concatenate(
            [jnp.concatenate([high, high], axis=1), jnp.concatenate([low, low], axis=1)], axis=0
        )
        product = dot(pairs[b], right, NT)
        scaled.append(product[:, :spread] + product[:, spread:])
    for b in range(blocks):
        product = folded(dot(tall(scaled[b]), pairs[b], NT))
        high, low = split(unit - jnp.where(b <= limit, product, 0.0))
        k_high[b] = high
        k_low[b] = low
    runs = blocks // run
    state, out = [None] * runs, [None] * runs
    for step in range(run):
        for j in range(runs):
            b = j * run + step
            high, low = k_high[b, :spread, :], k_low[b, :spread, :]
            if step == 0:
                both = high.astype(F32) + low.astype(F32)
            else:
                both = apply(state[j], high, low)
            state[j] = both[:, spread:]
            out[j] = both[:, :spread]
            high, low = split(out[j])
            q_high[j, :, step * spread : (step + 1) * spread] = high
            q_low[j, :, step * spread : (step + 1) * spread] = low
            if part == 0 and j == 0 and step < 2:
                first[:, step * spread : (step + 1) * spread] = out[j]
    for j in range(runs):
        maps[j] = state[j]
    if part == parts - 1:
        reach, total, last, final = refs
        every = [ref[j] for ref in earlier for j in range(runs)] + state
        so_far = every[0]
        for j in range(1, len(every)):
            reach[j - 1] = so_far
            if j == len(every) - 1:
                last[...] = out[-1]
                final[...] = times(so_far, out[-1])
            so_far = times(so_far, every[j])
        total[...] = so_far


class Sweep:
    def __init__(self, refl_v, sweep, parts, run):
        self.refl_v, self.sweep, self.parts, self.run = refl_v, sweep, parts, run
        self.high, self.low, self.q_high, self.q_low, self.maps = [], [], [], [], []

    def part(self):
        slots, double, spread = self.refl_v.shape[1:]
        part, count = len(self.maps), slots // self.parts
        runs = count // self.run
        shape = jax.ShapeDtypeStruct
        square = shape((spread, spread), F32)
        shapes = [shape((count, double, double), BF16)] * 2
        shapes += [shape((runs, spread, self.run * spread), BF16)] * 2
        shapes += [shape((runs, spread, spread), F32)]
        if part == 0:
            shapes.append(shape((spread, 2 * spread), F32))
        if part == self.parts - 1:
            every = slots // self.run
            shapes += [shape((every - 1, spread, spread), F32), square, square, square]
        last_slot = lax.axis_size("row") * slots - 3
        results = whole_call(
            functools.partial(
                reflect_kernel, self.run, self.sweep, part, self.parts, last_slot
            ),
            shapes, count * 500_000_000, [], [self.refl_v] + self.maps, vmem=16,
        )
        for kept, result in zip(
            (self.high, self.low, self.q_high, self.q_low, self.maps), results[:5]
        ):
            kept.append(result)
        rest = list(results[5:])
        if part == 0:
            self.first = rest.pop(0)
        if part == self.parts - 1:
            self.reach, self.total, self.last, self.final = rest
        return results


def merge_kernel(owners, cauchy, *refs):
    pieces, (merged, chosen) = refs[:-2], refs[-2:]
    rows, columns = pieces[0].shape
    mine = lax.axis_index("col")
    chosen[...] = rolled(cauchy[...], mine * rows)[:, : chosen.shape[1]]
    left = [
        chosen[pl.ds(pl.multiple_of((mine ^ owner) * rows, rows), rows), :rows] for owner in owners
    ]
    left_high, left_low = split(jnp.concatenate(left, axis=0))
    step = columns // 4
    for part in range(4):
        at = slice(part * step, (part + 1) * step)
        right_high, right_low = split(jnp.concatenate([piece[:, at] for piece in pieces], axis=0))
        merged[:, at] = dot(left_high, right_high, TN) + (
            dot(left_high, right_low, TN) + dot(left_low, right_high, TN)
        )


def shifted(array, by):
    devices = lax.axis_size("row")
    return lax.ppermute(array, "row", [(i, (i + by) % devices) for i in range(devices)])


def swapped(array, axis, distance):
    devices = lax.axis_size(axis)
    return lax.ppermute(array, axis, [(i, i ^ distance) for i in range(devices)])


def after_all(array, *others):
    return lax.optimization_barrier((array, *others))[0]


def rolled(value, left):
    width = value.shape[1]
    return pltpu.roll(value, lax.rem(width - left, width), 1)


def chain(first, aligned, parts, k, maps, y_local, joins, state):
    slots, rows, spread = y_local.shape
    per = slots // parts
    maps = [ref[j] for ref in maps for j in range(ref.shape[0])]
    runs = len(maps)
    run = slots // runs

    def segment(slot):
        return aligned[:, slot * spread : (slot + 1) * spread]

    carry = [jnp.zeros((rows, spread), F32)] * runs
    carry[0] = jnp.where(first, segment(0), 0.0)
    for step in range(run):
        for j in range(runs):
            slot = j * run + step
            fresh = jnp.concatenate([carry[j], segment(slot + 1)], axis=1)
            part, at = slot // per, slot % per
            both = apply(fresh, k[part][at], k[parts + part][at])
            y_local[slot] = both[:, :spread]
            carry[j] = both[:, spread:]
    so_far = carry[0]
    joins[0] = jnp.zeros_like(so_far)
    for j in range(1, runs):
        joins[j] = so_far
        so_far = times(so_far, maps[j]) + carry[j]
    state[...] = so_far


def first_kernel(parts, start, home, after, *refs):
    k, maps = refs[: 2 * parts], refs[2 * parts : 3 * parts]
    y_local, joins, state, head, front = refs[3 * parts :]
    slots, rows, spread = y_local.shape
    offset = start[0]
    head[...] = pltpu.roll(home[:, :spread], lax.rem(spread - offset, spread), 1)
    aligned = rolled(jnp.concatenate([home[...], after[:rows]], axis=1), offset)
    chain(lax.axis_index("row") == 0, aligned, parts, k, maps, y_local, joins, state)
    front[...] = y_local[:2]


def is_upper(level):
    return lax.rem(lax.axis_index("row") // (1 << level), 2) == 1


def join_maps_kernel(level, top, mine, other, *refs):
    upper = is_upper(level)
    if level:
        inner, refs = refs[0], refs[1:]
    if top:
        final, refs = refs[0], refs[1:]
    high, both, inside = refs[:3]
    low = jnp.where(upper, other[...], mine[...])
    high[...] = jnp.where(upper, mine[...], other[...])
    both[...] = times(low, high[...])
    if level:
        inside[...] = jnp.where(upper, times(low, inner[...]), inner[...])
    else:
        inside[...] = jnp.where(upper, low, eye(*low.shape).astype(F32))
    if top:
        refs[3][...] = jnp.where(is_upper(level + 1), times(inside[...], final[...]), 0.0)


def join_states_kernel(level, top, mine, other, high, *refs):
    upper = is_upper(level)
    if level:
        inner, before, refs = refs[0], refs[1], refs[2:]
    if top:
        tail, final, refs = refs[0], refs[1], refs[2:]
    low = jnp.where(upper, other[...], mine[...])
    refs[0][...] = times(low, high[...]) + jnp.where(upper, mine[...], other[...])
    if level:
        enters = before[...] + jnp.where(upper, times(low, inner[...]), 0.0)
    else:
        enters = jnp.where(upper, low, 0.0)
    refs[1][...] = enters
    if top:
        refs[2][...] = tail[...] + times(enters, final[...])


def join_maps(total, final=None):
    levels = lax.axis_size("row").bit_length() - 1
    square = jax.ShapeDtypeStruct(total.shape, F32)
    inside, found, seam = None, [], None
    for level in range(levels - 1):
        top = final is not None and level == levels - 2
        arrays = [total, swapped(total, "row", 1 << level)]
        arrays += ([inside] if level else []) + ([final] if top else [])
        high, total, inside, *seam = whole_call(
            functools.partial(join_maps_kernel, level, top), [square] * (4 if top else 3),
            100_000_000, [], arrays,
        )
        found.append((high, inside))
    return found, seam


def join_states(state, maps, tail=None, final=None):
    levels = len(maps) + 1
    segment = jax.ShapeDtypeStruct(state.shape, F32)
    enters, moved = None, None
    for level in range(levels - 1):
        top = tail is not None and level == levels - 2
        arrays = [state, swapped(state, "row", 1 << level), maps[level][0]]
        arrays += [maps[level - 1][1], enters] if level else []
        arrays += [tail, final] if top else []
        state, enters, *moved = whole_call(
            functools.partial(join_states_kernel, level, top), [segment] * (3 if top else 2),
            50_000_000, [], arrays,
        )
    return swapped(state, "row", 1 << (levels - 1)), enters, moved


def entering(levels, half, inner, before):
    enters = jnp.where(is_upper(levels - 1), half[...], 0.0)
    return enters, before[...] + times(enters, inner[...])


def settled(incoming, reach, joins, q, y_local, put):
    spread = incoming.shape[1]
    parts = len(q) // 2
    per, _, width = q[0].shape
    run = width // spread
    for j in range(parts * per):
        enters = incoming if j == 0 else joins[j] + times(incoming, reach[j - 1])
        part, at = j // per, j % per
        added = apply(enters, q[part][at], q[parts + part][at])
        for step in range(run):
            slot = j * run + step
            put(slot, y_local[slot] + added[:, step * spread : (step + 1) * spread])


def second_kernel(
    levels, parts_in, parts, start, half, inner, before, reach, joins_in, y_in, state_in, total_in,
    head, front, after, final, *refs,
):
    q, refs = refs[: 2 * parts_in], refs[2 * parts_in :]
    k, maps = refs[: 2 * parts], refs[2 * parts : 3 * parts]
    y_local, joins, state, head_out, tail, line = refs[3 * parts :]
    slots, rows, spread = y_local.shape
    incoming = entering(levels, half, inner, before)[1]

    def put(slot, value):
        line[:, (slot + 1) * spread : (slot + 2) * spread] = value

    line[:, :spread] = head[...]
    settled(incoming, reach, joins_in, q, y_in, put)
    leaving = times(incoming, total_in[...]) + state_in[...]
    added = times(leaving, after[rows:])
    for extra in range(2):
        put(slots + extra, front[extra] + added[:, extra * spread : (extra + 1) * spread])
    ahead = start[1] - start[0]
    head_out[...] = pltpu.roll(
        line[:, : 2 * spread], lax.rem(4 * spread - ahead, 2 * spread), 1
    )[:, :spread]
    aligned = rolled(line[...], ahead + spread)
    chain(lax.axis_index("row") == 0, aligned, parts, k, maps, y_local, joins, state)
    tail[...] = y_local[slots - 1] + times(joins[joins.shape[0] - 1], final[...])


def final_kernel(
    levels, parts, start, half, inner, before, reach, joins, y_local, head, tail, final, *refs
):
    q, (out, line) = refs[: 2 * parts], refs[2 * parts :]
    spread = head.shape[1]
    earlier, incoming = entering(levels, half, inner, before)

    def put(slot, value):
        line[:, (slot + 1) * spread : (slot + 2) * spread] = value

    line[:, :spread] = jnp.where(
        lax.axis_index("row") == 0, head[...], tail[...] + times(earlier, final[...])
    )
    settled(incoming, reach, joins, q, y_local, put)
    out[...] = rolled(line[...], spread - start[1])[:, : out.shape[1]]


def whole_call(kernel, shapes, flops, scalars, arrays, scratch=(), vmem=8):
    return pl.pallas_call(
        kernel,
        out_shape=shapes,
        in_specs=[SMEM] * len(scalars) + [VMEM] * len(arrays),
        out_specs=jax.tree.map(lambda shape: VMEM, shapes),
        scratch_shapes=list(scratch),
        compiler_params=pltpu.CompilerParams(vmem_limit_bytes=vmem << 20),
        cost_estimate=pl.CostEstimate(
            flops=flops, bytes_accessed=4_000_000, transcendentals=0
        ),
    )(*scalars, *arrays)


def run_length(slots):
    return next(size for size in (4, 2, 1) if slots % (2 * size) == 0)


def shards(panel, cauchy, refl_v, block_start):
    rows, columns = panel.shape
    slots, _, spread = refl_v.shape[1:]
    run = run_length(slots)
    levels = lax.axis_size("row").bit_length() - 1
    shape = functools.partial(jax.ShapeDtypeStruct, dtype=F32)
    segment = shape((rows, spread))
    chained = [shape((slots, rows, spread)), shape((slots // run, rows, spread)), segment]
    starts = [block_start]

    one = Sweep(refl_v, 0, 1, run)
    two = Sweep(refl_v, 1, 2, run)
    count = lax.axis_size("col")
    pieces, owners = [panel], [0]
    distance = count // 2
    while distance:
        pieces += [swapped(piece, "col", distance) for piece in pieces]
        if owners == [0]:
            one.part()
            pieces[-1] = after_all(pieces[-1], one.total)
        owners += [owner ^ distance for owner in owners]
        distance //= 2
    groups1, _ = join_maps(one.total)
    two.part()
    pieces[0] = after_all(pieces[0], two.maps[0], groups1[0][0])
    merged = whole_call(
        functools.partial(merge_kernel, owners), shape((rows, columns)),
        1_000_000_000, [], [cauchy] + pieces,
        [pltpu.VMEM((cauchy.shape[0], 128 * pl.cdiv(rows, 128)), F32)],
    )
    after = shifted(jnp.concatenate([merged[:, : 2 * spread], one.first], axis=0), -1)
    two.maps[0] = after_all(two.maps[0], merged)
    two.part()
    merged = after_all(merged, two.total)
    y1, joins1, state1, head1, front = whole_call(
        functools.partial(first_kernel, one.parts), chained + [segment, shape((2, rows, spread))],
        3_000_000_000, starts, [merged, after] + one.high + one.low + one.maps,
    )
    groups2, [seam] = join_maps(two.total, two.final)
    seam = shifted(seam, 1)
    front = shifted(front, -1)
    half1, enters1, _ = join_states(state1, groups1)
    y2, joins2, state2, head2, tail = whole_call(
        functools.partial(second_kernel, levels, one.parts, two.parts),
        chained + [segment, segment], 4_000_000_000, starts,
        [half1, groups1[-1][1], enters1, one.reach, joins1, y1, state1, one.total, head1, front,
         after, two.last] + one.q_high + one.q_low + two.high + two.low + two.maps,
        [pltpu.VMEM((rows, columns + 3 * spread), F32)],
    )
    half2, enters2, [tail] = join_states(state2, groups2, tail, two.final)
    tail = shifted(tail, 1)
    return whole_call(
        functools.partial(final_kernel, levels, two.parts), shape((rows, columns)), 1_000_000_000,
        starts,
        [half2, groups2[-1][1], enters2, two.reach, joins2, y2, head2, tail, seam]
        + two.q_high + two.q_low,
        [pltpu.VMEM((rows, columns + spread), F32)],
    )


def solution(mesh):
    placed = (P("col", "row"), P(), P(None, "row", None, None), P())
    return jax.shard_map(
        shards, mesh=mesh, in_specs=placed, out_specs=P("col", "row"), check_vma=False
    )
```

```python
import functools

import jax
import jax.numpy as jnp
from jax import lax
from jax.experimental import pallas as pl
from jax.experimental.pallas import tpu as pltpu
from jax.sharding import PartitionSpec as P

F32, BF16 = jnp.float32, jnp.bfloat16
VMEM = pl.BlockSpec(memory_space=pltpu.VMEM)
SMEM = pl.BlockSpec(memory_space=pltpu.SMEM)
NN = (((1,), (0,)), ((), ()))
NT = (((1,), (1,)), ((), ()))
TN = (((0,), (0,)), ((), ()))


def split(value):
    high = value.astype(BF16)
    return high, (value - high.astype(F32)).astype(BF16)


def dot(left, right, dims=NN):
    return lax.dot_general(left, right, dims, preferred_element_type=F32)


def wide(value):
    return jnp.concatenate(split(value), axis=1)


def tall(value):
    terms = [jnp.concatenate([term, term], axis=1) for term in split(value)]
    return jnp.concatenate(terms, axis=0)


def doubled(rows_high, rows_low):
    return jnp.concatenate([rows_high, rows_low], axis=0)


def folded(product):
    half = product.shape[0] // 2
    return product[:half] + product[half:]


def apply(left, high, low):
    if left.shape[1] <= 128:
        return folded(dot(tall(left), doubled(high, low)))
    left_high, left_low = split(left)
    return folded(dot(jnp.concatenate([left_high, left_low], axis=0), high)) + dot(left_high, low)


def times(left, right):
    return apply(left, *split(right))


def eye(rows, columns):
    shape = (rows, columns)
    return lax.broadcasted_iota(jnp.int32, shape, 0) == lax.broadcasted_iota(jnp.int32, shape, 1)


def upper_inverses(grams):
    spread = grams[0].shape[0]
    base = spread // 4
    diagonal = eye(spread, spread)
    above = lax.broadcasted_iota(jnp.int32, (spread, spread), 0) < lax.broadcasted_iota(
        jnp.int32, (spread, spread), 1
    )
    halves = [jnp.where(diagonal, 0.5 * gram, 0.0) for gram in grams]
    columns = [jnp.sum(half, axis=0, keepdims=True) for half in halves]
    scaled = [
        jnp.where(above, gram, 0.0) / jnp.sum(half, axis=1, keepdims=True)
        for gram, half in zip(grams, halves)
    ]

    def owner(size):
        return lax.broadcasted_iota(jnp.int32, (size, spread), 1) // size

    def compact(value, size, row=lambda block: block):
        owns = owner(size)
        result = value[row(0) * size : (row(0) + 1) * size]
        for block in range(1, spread // size):
            at = row(block) * size
            result = jnp.where(owns == block, value[at : at + size], result)
        return result

    def expanded(value, size, row=lambda block: block):
        owns = owner(size)
        masks = [(owns == block).astype(BF16) for block in range(spread // size)]
        terms = []
        for term in split(value):
            rows = [jnp.zeros_like(term)] * (spread // size)
            for block, mask in enumerate(masks):
                if row(block) is not None:
                    rows[row(block)] = term * mask
            terms.append(jnp.concatenate(rows, axis=0))
        return doubled(*terms)

    size = base
    unit = compact(diagonal.astype(F32), size)
    powers = [compact(value, size) for value in scaled]
    results = [unit - power for power in powers]
    rights = [expanded(power, size) for power in powers]
    powers = [folded(dot(tall(power), right)) for power, right in zip(powers, rights)]
    reach = 2
    while reach < size:
        reach *= 2
        rights = [expanded(power, size) for power in powers]
        if reach < size:
            lefts = [jnp.concatenate([r, p], axis=0) for r, p in zip(results, powers)]
        else:
            lefts = results
        products = [folded(dot(tall(left), right)) for left, right in zip(lefts, rights)]
        results = [result + product[:size] for result, product in zip(results, products)]
        if reach < size:
            powers = [product[size:] for product in products]
    while size < spread:
        odd = lax.rem(owner(size), 2) == 1
        edges = [
            jnp.where(odd, compact(value, size, lambda block: block & ~1), 0.0) for value in scaled
        ]
        rights = [expanded(result, size) for result in results]
        products = [folded(dot(tall(edge), right)) for edge, right in zip(edges, rights)]
        rights = [
            expanded(product, size, lambda block: block - 1 if block & 1 else None)
            for product in products
        ]
        products = [folded(dot(tall(result), right)) for result, right in zip(results, rights)]
        results = [
            jnp.concatenate(
                [jnp.where(odd, -product, result), jnp.where(odd, result, 0.0)], axis=0
            )
            for result, product in zip(results, products)
        ]
        size *= 2
    return [result / column for result, column in zip(results, columns)]


def reflect_kernel(run, sweeps, last_slot, source, *refs):
    count, double, spread = source.shape[1:]
    found = [refs[i * 8 : i * 8 + 8] for i in range(len(sweeps))]
    limit = last_slot - lax.axis_index("row") * count
    pairs = [wide(source[sweep, b]) for sweep in sweeps for b in range(count)]
    grams = [dot(pair, pair, TN) for pair in pairs]
    grams = [
        (g[:spread, :spread] + g[spread:, spread:]) + (g[:spread, spread:] + g[spread:, :spread])
        for g in grams
    ]
    triangles = upper_inverses(grams)
    unit = eye(double, double).astype(F32)
    scaled = []
    for pair, triangle in zip(pairs, triangles):
        high, low = split(triangle)
        right = jnp.concatenate(
            [jnp.concatenate([high, high], axis=1), jnp.concatenate([low, low], axis=1)], axis=0
        )
        product = dot(pair, right, NT)
        scaled.append(product[:, :spread] + product[:, spread:])
    for i, (pair, value) in enumerate(zip(pairs, scaled)):
        k_high, k_low = found[i // count][:2]
        product = folded(dot(tall(value), pair, NT))
        high, low = split(unit - jnp.where(i % count <= limit, product, 0.0))
        k_high[i % count] = high
        k_low[i % count] = low
    runs = count // run
    state, out = [[None] * runs for _ in found], [[None] * runs for _ in found]
    for step in range(run):
        for j in range(runs):
            for i, (k_high, k_low, q_high, q_low, _, _, _, first) in enumerate(found):
                b = j * run + step
                high, low = k_high[b, :spread, :], k_low[b, :spread, :]
                if step == 0:
                    both = high.astype(F32) + low.astype(F32)
                else:
                    both = apply(state[i][j], high, low)
                state[i][j] = both[:, spread:]
                out[i][j] = both[:, :spread]
                high, low = split(out[i][j])
                q_high[j, :, step * spread : (step + 1) * spread] = high
                q_low[j, :, step * spread : (step + 1) * spread] = low
                if j == 0 and step < 2:
                    first[:, step * spread : (step + 1) * spread] = out[i][j]
    so_far = [state[i][0] for i in range(len(found))]
    for j in range(runs):
        for i, (_, _, _, _, maps, reach, total, _) in enumerate(found):
            maps[j] = state[i][j]
            if j:
                reach[j - 1] = so_far[i]
                so_far[i] = times(so_far[i], state[i][j])
            if j == runs - 1:
                total[...] = so_far[i]


def reflect(refl_v, sweeps, run):
    slots, double, spread = refl_v.shape[1:]
    runs = slots // run
    shape = jax.ShapeDtypeStruct
    square = shape((spread, spread), F32)
    shapes = [shape((slots, double, double), BF16)] * 2
    shapes += [shape((runs, spread, run * spread), BF16)] * 2
    shapes += [shape((runs, spread, spread), F32), shape((runs - 1, spread, spread), F32), square]
    shapes += [shape((spread, 2 * spread), F32)]
    results = whole_call(
        functools.partial(reflect_kernel, run, sweeps, lax.axis_size("row") * slots - 3),
        shapes * len(sweeps), len(sweeps) * slots * 300_000_000, [], [refl_v], vmem=24,
    )
    return [results[i * 8 : i * 8 + 8] for i in range(len(sweeps))]


def merge_kernel(owners, cauchy, *refs):
    pieces, (merged, chosen) = refs[:-2], refs[-2:]
    rows, columns = pieces[0].shape
    mine = lax.axis_index("col")
    chosen[...] = rolled(cauchy[...], mine * rows)[:, : chosen.shape[1]]
    left = [
        chosen[pl.ds(pl.multiple_of((mine ^ owner) * rows, rows), rows), :rows] for owner in owners
    ]
    left_high, left_low = split(jnp.concatenate(left, axis=0))
    step = columns // 4
    for part in range(4):
        at = slice(part * step, (part + 1) * step)
        right_high, right_low = split(jnp.concatenate([piece[:, at] for piece in pieces], axis=0))
        merged[:, at] = dot(left_high, right_high, TN) + (
            dot(left_high, right_low, TN) + dot(left_low, right_high, TN)
        )


def shifted(array, by):
    devices = lax.axis_size("row")
    return lax.ppermute(array, "row", [(i, (i + by) % devices) for i in range(devices)])


def swapped(array, axis, distance):
    devices = lax.axis_size(axis)
    return lax.ppermute(array, axis, [(i, i ^ distance) for i in range(devices)])


def after_all(array, *others):
    return lax.optimization_barrier((array, *others))[0]


def rolled(value, left):
    width = value.shape[1]
    return pltpu.roll(value, lax.rem(width - left, width), 1)


def chain(first, aligned, k_high, k_low, maps, y_local, joins):
    slots, rows, spread = y_local.shape
    runs = maps.shape[0]
    run = slots // runs

    def segment(slot):
        return aligned[:, slot * spread : (slot + 1) * spread]

    carry = [jnp.zeros((rows, spread), F32)] * runs
    if first is not None:
        carry[0] = jnp.where(first, segment(0), 0.0)
    for step in range(run):
        for j in range(runs):
            slot = j * run + step
            fresh = jnp.concatenate([carry[j], segment(slot + 1)], axis=1)
            both = apply(fresh, k_high[slot], k_low[slot])
            y_local[slot] = both[:, :spread]
            carry[j] = both[:, spread:]
    so_far = carry[0]
    joins[0] = jnp.zeros_like(so_far)
    for j in range(1, runs):
        joins[j] = so_far
        so_far = times(so_far, maps[j]) + carry[j]
    return so_far


def first_kernel(start, home, after, k_high, k_low, maps, y_local, joins, state, head, front):
    slots, rows, spread = y_local.shape
    offset = start[0]
    head[...] = pltpu.roll(home[:, :spread], lax.rem(spread - offset, spread), 1)
    aligned = rolled(jnp.concatenate([home[...], after[...]], axis=1), offset)
    first = lax.axis_index("row") == 0
    state[...] = chain(first, aligned, k_high, k_low, maps, y_local, joins)
    front[...] = y_local[:2]


def settled(joins, q_high, q_low, y_local, put):
    runs, spread, width = q_high.shape
    run = width // spread
    for j in range(runs):
        added = apply(joins[j], q_high[j], q_low[j]) if j else None
        for step in range(run):
            slot = j * run + step
            value = y_local[slot]
            if j:
                value = value + added[:, step * spread : (step + 1) * spread]
            put(slot, value)


def line_kernel(head, joins, y_local, q_high, q_low, line):
    spread = head.shape[1]
    line[:, :spread] = head[...]

    def put(slot, value):
        line[:, (slot + 1) * spread : (slot + 2) * spread] = value

    settled(joins, q_high, q_low, y_local, put)


def second_kernel(
    start, ready, state_in, front, first_next, k_high, k_low, maps, y_local, joins, state, head,
    line,
):
    slots, rows, spread = y_local.shape
    width = ready.shape[1]
    line[:, :width] = ready[...]
    added = times(state_in[...], first_next[...])
    for extra in range(2):
        at = slice(extra * spread, (extra + 1) * spread)
        line[:, width + extra * spread : width + (extra + 1) * spread] = front[extra] + added[:, at]
    ahead = start[1] - start[0]
    head[...] = pltpu.roll(
        line[:, : 2 * spread], lax.rem(4 * spread - ahead, 2 * spread), 1
    )[:, :spread]
    first = lax.axis_index("row") == 0
    aligned = rolled(line[...], ahead + spread)
    state[:, :spread] = state_in[...]
    state[:, spread:] = chain(first, aligned, k_high, k_low, maps, y_local, joins)


def base_kernel(start, head, joins, y_local, q_high, q_low, base, tail, line):
    spread = head.shape[1]
    line[:, :spread] = jnp.where(lax.axis_index("row") == 0, head[...], 0.0)

    def put(slot, value):
        line[:, (slot + 1) * spread : (slot + 2) * spread] = value

    settled(joins, q_high, q_low, y_local, put)
    tail[...] = line[:, base.shape[1] :]
    base[...] = rolled(line[...], spread - start[1])[:, : base.shape[1]]


def response_kernel(
    start, q_high, q_low, reach, total, first_next, k_high, k_low, maps, y_local, joins, gamma, line
):
    runs, spread, width = q_high.shape
    line[:, :spread] = jnp.zeros((spread, spread), F32)
    for j in range(runs):
        if j:
            out = apply(reach[j - 1], q_high[j], q_low[j])
        else:
            out = q_high[j].astype(F32) + q_low[j].astype(F32)
        line[:, spread + j * width : spread + (j + 1) * width] = out
    line[:, spread + runs * width :] = times(total[...], first_next[...])
    aligned = rolled(line[...], start[1] - start[0] + spread)
    gamma[...] = chain(None, aligned, k_high, k_low, maps, y_local, joins)


def home_kernel(start, joins, y_local, q_high, q_low, reach, high, low, seam, line):
    runs, spread, width = q_high.shape
    columns = high.shape[1]
    line[:, :spread] = jnp.zeros((spread, spread), F32)

    def put(slot, value):
        line[:, (slot + 1) * spread : (slot + 2) * spread] = value

    for sweep in range(2):
        at = slice(sweep * spread, (sweep + 1) * spread)
        if sweep == 0:
            settled(joins, q_high, q_low, y_local, put)
        else:
            for j in range(runs):
                if j:
                    out = apply(reach[j - 1], q_high[j], q_low[j])
                else:
                    out = q_high[j].astype(F32) + q_low[j].astype(F32)
                line[:, spread + j * width : spread + (j + 1) * width] = out
        seam[at] = line[:, columns:]
        moved = split(rolled(line[...], spread - start[1])[:, :columns])
        high[at], low[at] = moved


def is_upper(level):
    return lax.rem(lax.axis_index("row") // (1 << level), 2) == 1


def through(states, maps):
    spread = maps.shape[1]
    first, second = states[:, :spread], states[:, spread:]
    return jnp.concatenate(
        [times(first, maps[0]), times(first, maps[1]) + times(second, maps[2])], axis=1
    )


def through_seam(states, seam):
    spread = seam.shape[1]
    return times(states[:, :spread], seam[:spread]) + times(states[:, spread:], seam[spread:])


def join_maps_kernel(level, mine, other, *refs):
    upper = is_upper(level)
    if level:
        inner, refs = refs[0], refs[1:]
    high, both, inside = refs
    spread = mine.shape[1]
    low = [jnp.where(upper, other[i], mine[i]) for i in range(3)]
    high[...] = jnp.where(upper, mine[...], other[...])

    def joined(later):
        return [
            times(low[0], later[0]),
            times(low[0], later[1]) + times(low[1], later[2]),
            times(low[2], later[2]),
        ]

    for i, value in enumerate(joined(high)):
        both[i] = value
    if level:
        for i, value in enumerate(joined(inner)):
            inside[i] = jnp.where(upper, value, inner[i])
    else:
        unit = eye(spread, spread).astype(F32)
        for i, value in enumerate([unit, jnp.zeros_like(unit), unit]):
            inside[i] = jnp.where(upper, low[i], value)


def seam_kernel(levels, inside, seam, out):
    spread = seam.shape[1]
    first, second = seam[:spread], seam[spread:]
    upper = is_upper(levels - 1)
    out[:spread] = jnp.where(upper, times(inside[0], first) + times(inside[1], second), 0.0)
    out[spread:] = jnp.where(upper, times(inside[2], second), 0.0)


def join_states_kernel(level, top, mine, other, high, *refs):
    upper = is_upper(level)
    if level:
        inner, before, refs = refs[0], refs[1], refs[2:]
    if top:
        tail, seam, refs = refs[0], refs[1], refs[2:]
    low = jnp.where(upper, other[...], mine[...])
    refs[0][...] = through(low, high) + jnp.where(upper, mine[...], other[...])
    if level:
        enters = before[...] + jnp.where(upper, through(low, inner), 0.0)
    else:
        enters = jnp.where(upper, low, 0.0)
    refs[1][...] = enters
    if top:
        refs[2][...] = tail[...] + through_seam(enters, seam)


def final_kernel(levels, start, half, inner, before, base, high, low, tail, seam, out):
    spread = tail.shape[1]
    enters = jnp.where(is_upper(levels - 1), half[...], 0.0)
    incoming = before[...] + through(enters, inner)
    out[...] = base[...] + apply(incoming, high[...], low[...])
    offset = start[1]
    lead = pltpu.roll(tail[...] + through_seam(enters, seam), offset, 1)
    column = lax.broadcasted_iota(jnp.int32, lead.shape, 1)
    kept = (column < offset) & (lax.axis_index("row") > 0)
    out[:, :spread] += jnp.where(kept, lead, 0.0)


def whole_call(kernel, shapes, flops, scalars, arrays, scratch=(), vmem=8):
    return pl.pallas_call(
        kernel,
        out_shape=shapes,
        in_specs=[SMEM] * len(scalars) + [VMEM] * len(arrays),
        out_specs=jax.tree.map(lambda shape: VMEM, shapes),
        scratch_shapes=list(scratch),
        compiler_params=pltpu.CompilerParams(vmem_limit_bytes=vmem << 20),
        cost_estimate=pl.CostEstimate(
            flops=flops, bytes_accessed=4_000_000, transcendentals=0
        ),
    )(*scalars, *arrays)


def run_length(slots):
    return next(size for size in (4, 2, 1) if slots % (2 * size) == 0)


def shards(panel, cauchy, refl_v, block_start):
    rows, columns = panel.shape
    slots, _, spread = refl_v.shape[1:]
    run = run_length(slots)
    levels = lax.axis_size("row").bit_length() - 1
    shape = functools.partial(jax.ShapeDtypeStruct, dtype=F32)
    segment = shape((rows, spread))
    chained = [shape((slots, rows, spread)), shape((slots // run, rows, spread)), segment]
    starts = [block_start]

    count = lax.axis_size("col")
    pieces, owners = [panel], [0]
    distance = count // 2
    while distance:
        pieces += [swapped(piece, "col", distance) for piece in pieces]
        if owners == [0]:
            if slots <= 16:
                one, two = reflect(refl_v, (0, 1), run)
            else:
                [one], [two] = reflect(refl_v, (0,), run), reflect(refl_v, (1,), run)
            high1, low1, qh1, ql1, maps1, reach1, total1, first1 = one
            high2, low2, qh2, ql2, maps2, reach2, total2, _ = two
            pieces[-1] = after_all(pieces[-1], total1)
        owners += [owner ^ distance for owner in owners]
        distance //= 2
    first_next = shifted(first1, -1)
    merged = whole_call(
        functools.partial(merge_kernel, owners), shape((rows, columns)),
        1_000_000_000, [], [cauchy] + pieces,
        [pltpu.VMEM((cauchy.shape[0], 128 * pl.cdiv(rows, 128)), F32)],
    )
    after = shifted(merged[:, : 2 * spread], -1)

    square = shape((spread, spread))
    long = columns + 3 * spread
    responses = [
        shape((slots, spread, spread)), shape((slots // run, spread, spread)), square
    ]
    y_response, joins_response, gamma = whole_call(
        response_kernel, responses, 4_000_000_000, starts,
        [qh1, ql1, reach1, after_all(total1, merged), first_next, high2, low2, maps2],
        [pltpu.VMEM((spread, long), F32)],
    )
    maps = jnp.stack([total1, gamma, total2])
    groups, inside = [], None
    for level in range(levels - 1):
        arrays = [maps, swapped(maps, "row", 1 << level)] + ([inside] if level else [])
        high, maps, inside = whole_call(
            functools.partial(join_maps_kernel, level), [shape(maps.shape)] * 3, 400_000_000, [],
            arrays,
        )
        groups.append((high, inside))

    y1, joins1, state1, head1, front = whole_call(
        first_kernel, chained + [segment, shape((2, rows, spread))], 3_000_000_000, starts,
        [after_all(merged, gamma), after, high1, low1, maps1],
    )
    front = shifted(front, -1)
    line = whole_call(
        line_kernel, shape((rows, columns + spread)), 1_000_000_000, [],
        [head1, joins1, y1, qh1, ql1],
    )
    states = shape((rows, 2 * spread))
    y2, joins2, state, head2 = whole_call(
        second_kernel, chained[:2] + [states, segment], 3_000_000_000, starts,
        [line, state1, front, first_next, high2, low2, maps2],
        [pltpu.VMEM((rows, long), F32)],
    )
    base, tail = whole_call(
        base_kernel, [shape((rows, columns)), segment], 2_000_000_000, starts,
        [head2, joins2, y2, qh2, ql2], [pltpu.VMEM((rows, columns + spread), F32)],
    )
    home = jax.ShapeDtypeStruct((2 * spread, columns), BF16)
    home_high, home_low, seam = whole_call(
        home_kernel, [home, home, shape((2 * spread, spread))], 3_000_000_000, starts,
        [joins_response, y_response, qh2, ql2, reach2],
        [pltpu.VMEM((spread, columns + spread), F32)],
    )
    seam_far = whole_call(
        functools.partial(seam_kernel, levels), shape(seam.shape), 100_000_000, [],
        [groups[-1][1], seam],
    )
    seam_far = shifted(seam_far, 1)

    enters = None
    for level in range(levels - 1):
        top = level == levels - 2
        arrays = [state, swapped(state, "row", 1 << level), groups[level][0]]
        arrays += [groups[level - 1][1], enters] if level else []
        arrays += [tail, seam] if top else []
        state, enters, *moved = whole_call(
            functools.partial(join_states_kernel, level, top),
            [states] * 2 + [segment] * top, 100_000_000, [], arrays,
        )
    half = swapped(state, "row", 1 << (levels - 1))
    tail = shifted(moved[0], 1)
    return whole_call(
        functools.partial(final_kernel, levels), shape((rows, columns)), 1_000_000_000, starts,
        [half, groups[-1][1], enters, base, home_high, home_low, tail, seam_far],
    )


def solution(mesh):
    placed = (P("col", "row"), P(), P(None, "row", None, None), P())
    return jax.shard_map(
        shards, mesh=mesh, in_specs=placed, out_specs=P("col", "row"), check_vma=False
    )
```

```python
import functools

import jax
import jax.numpy as jnp
from jax import lax
from jax.experimental import pallas as pl
from jax.experimental.pallas import tpu as pltpu
from jax.sharding import PartitionSpec as P

F32, BF16 = jnp.float32, jnp.bfloat16
VMEM = pl.BlockSpec(memory_space=pltpu.VMEM)
SMEM = pl.BlockSpec(memory_space=pltpu.SMEM)
NN = (((1,), (0,)), ((), ()))
NT = (((1,), (1,)), ((), ()))
TN = (((0,), (0,)), ((), ()))


def split(value):
    high = value.astype(BF16)
    return high, (value - high.astype(F32)).astype(BF16)


def dot(left, right, dims=NN):
    return lax.dot_general(left, right, dims, preferred_element_type=F32)


def wide(value):
    return jnp.concatenate(split(value), axis=1)


def tall(value):
    terms = [jnp.concatenate([term, term], axis=1) for term in split(value)]
    return jnp.concatenate(terms, axis=0)


def doubled(rows_high, rows_low):
    return jnp.concatenate([rows_high, rows_low], axis=0)


def folded(product):
    half = product.shape[0] // 2
    return product[:half] + product[half:]


def apply(left, high, low):
    if left.shape[1] <= 128:
        return folded(dot(tall(left), doubled(high, low)))
    left_high, left_low = split(left)
    return folded(dot(jnp.concatenate([left_high, left_low], axis=0), high)) + dot(left_high, low)


def times(left, right):
    return apply(left, *split(right))


def eye(rows, columns):
    shape = (rows, columns)
    return lax.broadcasted_iota(jnp.int32, shape, 0) == lax.broadcasted_iota(jnp.int32, shape, 1)


def upper_inverses(grams):
    spread = grams[0].shape[0]
    base = spread // 4
    diagonal = eye(spread, spread)
    above = lax.broadcasted_iota(jnp.int32, (spread, spread), 0) < lax.broadcasted_iota(
        jnp.int32, (spread, spread), 1
    )
    halves = [jnp.where(diagonal, 0.5 * gram, 0.0) for gram in grams]
    columns = [jnp.sum(half, axis=0, keepdims=True) for half in halves]
    scaled = [
        jnp.where(above, gram, 0.0) / jnp.sum(half, axis=1, keepdims=True)
        for gram, half in zip(grams, halves)
    ]

    def owner(size):
        return lax.broadcasted_iota(jnp.int32, (size, spread), 1) // size

    def compact(value, size, row=lambda block: block):
        owns = owner(size)
        result = value[row(0) * size : (row(0) + 1) * size]
        for block in range(1, spread // size):
            at = row(block) * size
            result = jnp.where(owns == block, value[at : at + size], result)
        return result

    def expanded(value, size, row=lambda block: block):
        owns = owner(size)
        masks = [(owns == block).astype(BF16) for block in range(spread // size)]
        terms = []
        for term in split(value):
            rows = [jnp.zeros_like(term)] * (spread // size)
            for block, mask in enumerate(masks):
                if row(block) is not None:
                    rows[row(block)] = term * mask
            terms.append(jnp.concatenate(rows, axis=0))
        return doubled(*terms)

    size = base
    unit = compact(diagonal.astype(F32), size)
    powers = [compact(value, size) for value in scaled]
    results = [unit - power for power in powers]
    rights = [expanded(power, size) for power in powers]
    powers = [folded(dot(tall(power), right)) for power, right in zip(powers, rights)]
    reach = 2
    while reach < size:
        reach *= 2
        rights = [expanded(power, size) for power in powers]
        if reach < size:
            lefts = [jnp.concatenate([r, p], axis=0) for r, p in zip(results, powers)]
        else:
            lefts = results
        products = [folded(dot(tall(left), right)) for left, right in zip(lefts, rights)]
        results = [result + product[:size] for result, product in zip(results, products)]
        if reach < size:
            powers = [product[size:] for product in products]
    while size < spread:
        odd = lax.rem(owner(size), 2) == 1
        edges = [
            jnp.where(odd, compact(value, size, lambda block: block & ~1), 0.0) for value in scaled
        ]
        rights = [expanded(result, size) for result in results]
        products = [folded(dot(tall(edge), right)) for edge, right in zip(edges, rights)]
        rights = [
            expanded(product, size, lambda block: block - 1 if block & 1 else None)
            for product in products
        ]
        products = [folded(dot(tall(result), right)) for result, right in zip(results, rights)]
        results = [
            jnp.concatenate(
                [jnp.where(odd, -product, result), jnp.where(odd, result, 0.0)], axis=0
            )
            for result, product in zip(results, products)
        ]
        size *= 2
    return [result / column for result, column in zip(results, columns)]


def reflectors(values, active):
    double, spread = values[0].shape
    pairs = [wide(value) for value in values]
    grams = [dot(pair, pair, TN) for pair in pairs]
    grams = [
        (g[:spread, :spread] + g[spread:, spread:]) + (g[:spread, spread:] + g[spread:, :spread])
        for g in grams
    ]
    triangles = upper_inverses(grams)
    unit = eye(double, double).astype(F32)
    scaled = []
    for pair, triangle in zip(pairs, triangles):
        high, low = split(triangle)
        right = jnp.concatenate(
            [jnp.concatenate([high, high], axis=1), jnp.concatenate([low, low], axis=1)], axis=0
        )
        product = dot(pair, right, NT)
        scaled.append(product[:, :spread] + product[:, spread:])
    for pair, value, kept in zip(pairs, scaled, active):
        product = folded(dot(tall(value), pair, NT))
        yield split(unit - jnp.where(kept, product, 0.0))


def runs_of(slots, extra=0):
    size = next(size for size in (4, 2, 1) if slots % size == 0)
    bounds = [0, 1] + list(range(size, slots + 1, size)) if size > 1 else list(range(slots + 1))
    runs = list(zip(bounds[:-1], bounds[1:]))
    runs[-1] = (runs[-1][0], runs[-1][1] + extra)
    return runs


def edges_kernel(source, last, first):
    last[...] = source[:, source.shape[1] - 1]
    first[...] = source[0, :2]


def reflect_kernel(sweeps, last_slot, source, *refs):
    count, double, spread = source.shape[1:]
    found = [refs[i * 7 : i * 7 + 7] for i in range(len(sweeps))]
    limit = last_slot - lax.axis_index("row") * count
    values = [source[sweep, b] for sweep in sweeps for b in range(count)]
    active = [b <= limit for _ in sweeps for b in range(count)]
    for i, (high, low) in enumerate(reflectors(values, active)):
        found[i // count][0][i % count] = high
        found[i // count][1][i % count] = low
    runs = runs_of(count, 1)[1:]
    state = [[None] * len(runs) for _ in found]
    for step in range(max(stop - at for at, stop in runs)):
        for j, (at, stop) in enumerate(runs):
            if at + step >= stop:
                continue
            for i, (k_high, k_low, q_high, q_low, maps, upto, beyond) in enumerate(found):
                b = at + step - 1
                high, low = k_high[b, :spread, :], k_low[b, :spread, :]
                if step == 0:
                    both = high.astype(F32) + low.astype(F32)
                else:
                    both = apply(state[i][j], high, low)
                state[i][j] = both[:, spread:]
                q_high[b], q_low[b] = split(both[:, :spread])
                if b == count - 2 or (at + step + 1 == stop and b < count - 1):
                    maps[j] = both[:, spread:]
                if b == count - 1:
                    beyond[...] = both[:, spread:]
    for i, (_, _, _, _, maps, upto, _) in enumerate(found):
        so_far = maps[0]
        upto[0] = so_far
        for j in range(1, len(runs)):
            so_far = times(so_far, maps[j])
            upto[j] = so_far


def reflect(refl_v, sweeps):
    slots, double, spread = refl_v.shape[1:]
    runs = len(runs_of(slots)) - 1
    shape = jax.ShapeDtypeStruct
    shapes = [shape((slots, double, double), BF16)] * 2
    shapes += [shape((slots, spread, spread), BF16)] * 2
    shapes += [shape((runs, spread, spread), F32)] * 2 + [shape((spread, spread), F32)]
    results = whole_call(
        functools.partial(reflect_kernel, sweeps, lax.axis_size("row") * slots - 3),
        shapes * len(sweeps), len(sweeps) * slots * 300_000_000, [], [refl_v], vmem=24,
    )
    return [results[i * 7 : i * 7 + 7] for i in range(len(sweeps))]


def edge_kernel(
    count, last_slot, left, right, upto1, upto2, beyond, left_high, left_low, right_high, right_low,
    q_high, q_low, reach, total,
):
    sweeps, _, spread = left.shape
    extra = right.shape[0]
    first = lax.axis_index("row") * count
    values = [left[i] for i in range(sweeps)] + [right[i] for i in range(extra)]
    active = [(first > 0) & (first - 1 <= last_slot)] * sweeps
    active += [first + count + i <= last_slot for i in range(extra)]
    for i, (high, low) in enumerate(reflectors(values, active)):
        if i < sweeps:
            left_high[i], left_low[i] = high, low
        else:
            right_high[i - sweeps], right_low[i - sweeps] = high, low
    state = beyond[...]
    for i in range(extra):
        both = apply(state, right_high[i, :spread, :], right_low[i, :spread, :])
        q_high[i], q_low[i] = split(both[:, :spread])
        state = both[:, spread:]
    for i, upto in enumerate((upto1, upto2)):
        entry = left_high[i, :spread, spread:].astype(F32) + left_low[i, :spread, spread:].astype(F32)
        reach[i, 0] = entry
        for j in range(upto.shape[0] - 1):
            reach[i, j + 1] = times(entry, upto[j])
        total[i] = times(entry, upto[upto.shape[0] - 1])


def merge_kernel(owners, cauchy, *refs):
    pieces, (merged, chosen) = refs[:-2], refs[-2:]
    rows, columns = pieces[0].shape
    mine = lax.axis_index("col")
    chosen[...] = rolled(cauchy[...], mine * rows)[:, : chosen.shape[1]]
    left = [
        chosen[pl.ds(pl.multiple_of((mine ^ owner) * rows, rows), rows), :rows] for owner in owners
    ]
    left_high, left_low = split(jnp.concatenate(left, axis=0))
    step = columns // 4
    for part in range(4):
        at = slice(part * step, (part + 1) * step)
        right_high, right_low = split(jnp.concatenate([piece[:, at] for piece in pieces], axis=0))
        merged[:, at] = dot(left_high, right_high, TN) + (
            dot(left_high, right_low, TN) + dot(left_low, right_high, TN)
        )


def shifted(array, by):
    devices = lax.axis_size("row")
    return lax.ppermute(array, "row", [(i, (i + by) % devices) for i in range(devices)])


def swapped(array, axis, distance):
    devices = lax.axis_size(axis)
    return lax.ppermute(array, axis, [(i, i ^ distance) for i in range(devices)])


def after_all(array, *others):
    return lax.optimization_barrier((array, *others))[0]


def rolled(value, left):
    width = value.shape[1]
    return pltpu.roll(value, lax.rem(width - left, width), 1)


def slot_table(left, own, right=None):
    (left_ref, at), extra = left, 0 if right is None else right.shape[0]
    table = [(left_ref, at)] + [(own, b) for b in range(own.shape[0])]
    return table + [(right, b) for b in range(extra)]


def chain(aligned, k_high, k_low, runs, maps, slots, y_local, joins):
    rows, spread = joins.shape[1:]
    carry = [jnp.zeros((rows, spread), F32)] * len(runs)
    ends = [None] * len(runs)
    for step in range(max(stop - at for at, stop in runs)):
        for j, (at, stop) in enumerate(runs):
            slot = at + step
            if slot >= stop:
                continue
            fresh = aligned[:, slot * spread : (slot + 1) * spread]
            (high, b), (low, _) = k_high[slot], k_low[slot]
            both = apply(jnp.concatenate([carry[j], fresh], axis=1), high[b], low[b])
            y_local[slot] = both[:, :spread]
            carry[j] = both[:, spread:]
            if slot + 1 == min(stop, slots):
                ends[j] = carry[j]
    joins[0] = jnp.zeros_like(carry[0])
    so_far = ends[0]
    for j in range(1, len(runs)):
        joins[j] = so_far
        so_far = times(so_far, maps[j - 1]) + ends[j]
    return so_far


def terms(table, runs):
    return [jnp.concatenate([ref[b] for ref, b in table[at:stop]], axis=1) for at, stop in runs]


def settled(runs, joins, q_high, q_low, y_local, line):
    spread = y_local.shape[2]
    highs, lows = terms(q_high, runs[1:]), terms(q_low, runs[1:])
    for j, (at, stop) in enumerate(runs):
        added = apply(joins[j], highs[j - 1], lows[j - 1]) if j else None
        for slot in range(at, stop):
            value = y_local[slot]
            if j:
                value = value + added[:, (slot - at) * spread : (slot - at + 1) * spread]
            line[:, slot * spread : (slot + 1) * spread] = value


def reached(runs, entry, reach, q_high, q_low, line):
    spread = entry.shape[0]
    line[:, :spread] = entry
    highs, lows = terms(q_high, runs[1:]), terms(q_low, runs[1:])
    for j, (at, stop) in enumerate(runs[1:]):
        line[:, at * spread : stop * spread] = apply(reach[j], highs[j], lows[j])


def first_kernel(
    count, start, home, after, left_high, left_low, k_high, k_low, right_high, right_low, maps,
    q_high, q_low, q_right_high, q_right_low, line, state, y_local, joins,
):
    spread = state.shape[1]
    offset = start[0]
    aligned = rolled(jnp.concatenate([home[...], after[...]], axis=1), offset)
    runs = runs_of(count, y_local.shape[0] - count)
    highs = slot_table((left_high, 0), k_high, right_high)
    lows = slot_table((left_low, 0), k_low, right_low)
    state[...] = chain(aligned, highs, lows, runs, maps, count, y_local, joins)
    q_highs = slot_table((None, 0), q_high, q_right_high)
    q_lows = slot_table((None, 0), q_low, q_right_low)
    settled(runs, joins, q_highs, q_lows, y_local, line)

    @pl.when(lax.axis_index("row") == 0)
    def _():
        line[:, :spread] = pltpu.roll(home[:, :spread], lax.rem(spread - offset, spread), 1)


def second_kernel(
    count, start, line, state_in, left_high, left_low, k_high, k_low, maps, y_local, joins, state,
    head,
):
    spread = head.shape[1]
    ahead = start[1] - start[0]
    aligned = rolled(line[...], ahead + spread)
    runs = runs_of(count, y_local.shape[0] - count)
    highs, lows = slot_table((left_high, 1), k_high), slot_table((left_low, 1), k_low)
    state[:, spread:] = chain(aligned, highs, lows, runs, maps, count, y_local, joins)
    state[:, :spread] = state_in[...]
    head[...] = pltpu.roll(
        line[:, : 2 * spread], lax.rem(4 * spread - ahead, 2 * spread), 1
    )[:, :spread]


def base_kernel(count, start, head, joins, y_local, q_high, q_low, base, line):
    spread = head.shape[1]
    runs = runs_of(count, y_local.shape[0] - count)
    q_highs, q_lows = slot_table((None, 0), q_high), slot_table((None, 0), q_low)
    settled(runs, joins, q_highs, q_lows, y_local, line)

    @pl.when(lax.axis_index("row") == 0)
    def _():
        line[:, :spread] = head[...]

    base[...] = rolled(line[...], spread - start[1])[:, : base.shape[1]]


def response_kernel(
    count, start, q_high, q_low, q_right_high, q_right_low, reach, left_high, left_low, k_high,
    k_low, maps, y_local, joins, gamma, line,
):
    spread = gamma.shape[0]
    entry = left_high[0, :spread, :spread].astype(F32) + left_low[0, :spread, :spread].astype(F32)
    q_highs = slot_table((None, 0), q_high, q_right_high)
    q_lows = slot_table((None, 0), q_low, q_right_low)
    reached(runs_of(count, line.shape[1] // spread - count), entry, reach.at[0], q_highs, q_lows, line)
    aligned = rolled(line[...], start[1] - start[0] + spread)
    runs = runs_of(count, y_local.shape[0] - count)
    highs, lows = slot_table((left_high, 1), k_high), slot_table((left_low, 1), k_low)
    gamma[...] = chain(aligned, highs, lows, runs, maps, count, y_local, joins)


def home_kernel(
    count, start, joins, y_local, q_high, q_low, reach, left_high, left_low, high, low, line
):
    spread, columns = line.shape[0], high.shape[1]
    runs = runs_of(count, y_local.shape[0] - count)
    q_highs, q_lows = slot_table((None, 0), q_high), slot_table((None, 0), q_low)
    for sweep in range(2):
        at = slice(sweep * spread, (sweep + 1) * spread)
        if sweep == 0:
            settled(runs, joins, q_highs, q_lows, y_local, line)
        else:
            entry = left_high[1, :spread, :spread].astype(F32)
            entry = entry + left_low[1, :spread, :spread].astype(F32)
            reached(runs, entry, reach.at[1], q_highs, q_lows, line)
        high[at], low[at] = split(rolled(line[...], spread - start[1])[:, :columns])


def is_upper(level):
    return lax.rem(lax.axis_index("row") // (1 << level), 2) == 1


def through(states, maps):
    spread = maps.shape[1]
    first, second = states[:, :spread], states[:, spread:]
    return jnp.concatenate(
        [times(first, maps[0]), times(first, maps[1]) + times(second, maps[2])], axis=1
    )


def join_maps_kernel(level, *refs):
    upper = is_upper(level)
    if level:
        mine, other, inner, high, both, inside = refs
        mine, other = [mine[i] for i in range(3)], [other[i] for i in range(3)]
    else:
        mine, gamma, other, gamma_other, high, both, inside = refs
        mine, other = [mine[0], gamma[...], mine[1]], [other[0], gamma_other[...], other[1]]
    spread = both.shape[1]
    low = [jnp.where(upper, other[i], mine[i]) for i in range(3)]
    for i in range(3):
        high[i] = jnp.where(upper, mine[i], other[i])

    def joined(later):
        return [
            times(low[0], later[0]),
            times(low[0], later[1]) + times(low[1], later[2]),
            times(low[2], later[2]),
        ]

    for i, value in enumerate(joined(high)):
        both[i] = value
    if level:
        for i, value in enumerate(joined(inner)):
            inside[i] = jnp.where(upper, value, inner[i])
    else:
        unit = eye(spread, spread).astype(F32)
        for i, value in enumerate([unit, jnp.zeros_like(unit), unit]):
            inside[i] = jnp.where(upper, low[i], value)


def join_states_kernel(level, mine, other, high, *refs):
    upper = is_upper(level)
    if level:
        inner, before, refs = refs[0], refs[1], refs[2:]
    low = jnp.where(upper, other[...], mine[...])
    refs[0][...] = through(low, high) + jnp.where(upper, mine[...], other[...])
    if level:
        refs[1][...] = before[...] + jnp.where(upper, through(low, inner), 0.0)
    else:
        refs[1][...] = jnp.where(upper, low, 0.0)


def final_kernel(levels, half, inner, before, base, high, low, out):
    enters = jnp.where(is_upper(levels - 1), half[...], 0.0)
    incoming = before[...] + through(enters, inner)
    out[...] = base[...] + apply(incoming, high[...], low[...])


def whole_call(kernel, shapes, flops, scalars, arrays, scratch=(), vmem=8):
    return pl.pallas_call(
        kernel,
        out_shape=shapes,
        in_specs=[SMEM] * len(scalars) + [VMEM] * len(arrays),
        out_specs=jax.tree.map(lambda shape: VMEM, shapes),
        scratch_shapes=list(scratch),
        compiler_params=pltpu.CompilerParams(vmem_limit_bytes=vmem << 20),
        cost_estimate=pl.CostEstimate(
            flops=flops, bytes_accessed=4_000_000, transcendentals=0
        ),
    )(*scalars, *arrays)


def shards(panel, cauchy, refl_v, block_start):
    rows, columns = panel.shape
    slots, _, spread = refl_v.shape[1:]
    levels = lax.axis_size("row").bit_length() - 1
    last_slot = lax.axis_size("row") * slots - 3
    shape = functools.partial(jax.ShapeDtypeStruct, dtype=F32)
    starts = [block_start]
    count, runs = lax.axis_size("col"), len(runs_of(slots))
    square = (spread, spread)

    pieces, owners = [panel], [0]
    distance = count // 2
    while distance:
        pieces += [swapped(piece, "col", distance) for piece in pieces]
        if owners == [0]:
            pair = shape((2,) + refl_v.shape[2:])
            left, right = whole_call(edges_kernel, [pair, pair], 10_000_000, [], [refl_v])
            left, right = shifted(left, 1), shifted(right, -1)
            if slots <= 16:
                one, two = reflect(refl_v, (0, 1))
            else:
                [one], [two] = reflect(refl_v, (0,)), reflect(refl_v, (1,))
            high1, low1, qh1, ql1, maps1, upto1, beyond = one
            high2, low2, qh2, ql2, maps2, upto2, _ = two
            pieces[-1] = after_all(pieces[-1], beyond, left, right)
        owners += [owner ^ distance for owner in owners]
        distance //= 2
    k_pair = jax.ShapeDtypeStruct((2,) + (2 * spread, 2 * spread), BF16)
    q_pair = jax.ShapeDtypeStruct((2,) + square, BF16)
    lh, ll, rh, rl, qrh, qrl, reach, totals = whole_call(
        functools.partial(edge_kernel, slots, last_slot),
        [k_pair] * 4 + [q_pair] * 2 + [shape((2, runs - 1) + square), shape((2,) + square)],
        2_000_000_000, [], [left, right, upto1, upto2, beyond],
    )
    totals_other = swapped(totals, "row", 1)
    pieces[0] = after_all(pieces[0], totals)
    merged = whole_call(
        functools.partial(merge_kernel, owners), shape((rows, columns)),
        1_000_000_000, [], [cauchy] + pieces,
        [pltpu.VMEM((cauchy.shape[0], 128 * pl.cdiv(rows, 128)), F32)],
    )
    after = shifted(merged[:, : 4 * spread], -1)

    y_response, joins_response, gamma = whole_call(
        functools.partial(response_kernel, slots),
        [shape((slots + 1,) + square), shape((runs,) + square), shape(square)],
        4_000_000_000, starts,
        [qh1, ql1, qrh, qrl, after_all(reach, merged), lh, ll, high2, low2, maps2],
        [pltpu.VMEM((spread, columns + 3 * spread), F32)],
    )
    line, state1 = whole_call(
        functools.partial(first_kernel, slots),
        [shape((rows, columns + 3 * spread)), shape((rows, spread))], 3_000_000_000, starts,
        [after_all(merged, gamma), after, lh, ll, high1, low1, rh, rl, maps1, qh1, ql1, qrh, qrl],
        [pltpu.VMEM((slots + 3, rows, spread), F32), pltpu.VMEM((runs, rows, spread), F32)],
    )
    groups = []
    for level in range(levels - 1):
        if level:
            arrays = [maps, swapped(maps, "row", 1 << level), inside]
        else:
            arrays = [after_all(totals, state1), gamma, totals_other, swapped(gamma, "row", 1)]
        high, maps, inside = whole_call(
            functools.partial(join_maps_kernel, level), [shape((3,) + square)] * 3,
            400_000_000, [], arrays,
        )
        groups.append((high, inside))

    states = shape((rows, 2 * spread))
    y2, joins2, state, head2 = whole_call(
        functools.partial(second_kernel, slots),
        [shape((slots + 1, rows, spread)), shape((runs, rows, spread)), states,
         shape((rows, spread))],
        3_000_000_000, starts,
        [after_all(line, groups[0][0]), state1, lh, ll, high2, low2, maps2],
    )
    home = jax.ShapeDtypeStruct((2 * spread, columns), BF16)
    home_high, home_low = whole_call(
        functools.partial(home_kernel, slots), [home, home], 3_000_000_000, starts,
        [after_all(joins_response, state), y_response, qh2, ql2, reach, lh, ll],
        [pltpu.VMEM((spread, columns + spread), F32)],
    )
    base = whole_call(
        functools.partial(base_kernel, slots), shape((rows, columns)), 2_000_000_000, starts,
        [head2, joins2, y2, qh2, ql2], [pltpu.VMEM((rows, columns + spread), F32)],
    )
    enters = None
    for level in range(levels - 1):
        other = after_all(swapped(state, "row", 1 << level), groups[-1][0])
        arrays = [state, other, groups[level][0]]
        arrays += [groups[level - 1][1], enters] if level else []
        state, enters = whole_call(
            functools.partial(join_states_kernel, level), [states] * 2, 100_000_000, [], arrays,
        )
    half = swapped(state, "row", 1 << (levels - 1))
    return whole_call(
        functools.partial(final_kernel, levels), shape((rows, columns)), 1_000_000_000, [],
        [half, groups[-1][1], enters, base, home_high, home_low],
    )


def solution(mesh):
    placed = (P("col", "row"), P(), P(None, "row", None, None), P())
    return jax.shard_map(
        shards, mesh=mesh, in_specs=placed, out_specs=P("col", "row"), check_vma=False
    )
```

```python
import functools

import jax
import jax.numpy as jnp
from jax import lax
from jax.experimental import pallas as pl
from jax.experimental.pallas import tpu as pltpu
from jax.sharding import PartitionSpec as P

F32, BF16 = jnp.float32, jnp.bfloat16
VMEM = pl.BlockSpec(memory_space=pltpu.VMEM)
SMEM = pl.BlockSpec(memory_space=pltpu.SMEM)
NN = (((1,), (0,)), ((), ()))
NT = (((1,), (1,)), ((), ()))
TN = (((0,), (0,)), ((), ()))


def split(value):
    high = value.astype(BF16)
    return high, (value - high.astype(F32)).astype(BF16)


def dot(left, right, dims=NN):
    return lax.dot_general(left, right, dims, preferred_element_type=F32)


def wide(value):
    return jnp.concatenate(split(value), axis=1)


def tall(value):
    terms = [jnp.concatenate([term, term], axis=1) for term in split(value)]
    return jnp.concatenate(terms, axis=0)


def doubled(rows_high, rows_low):
    return jnp.concatenate([rows_high, rows_low], axis=0)


def folded(product):
    half = product.shape[0] // 2
    return product[:half] + product[half:]


def apply(left, high, low):
    if left.shape[1] <= 128:
        return folded(dot(tall(left), doubled(high, low)))
    left_high, left_low = split(left)
    return folded(dot(jnp.concatenate([left_high, left_low], axis=0), high)) + dot(left_high, low)


def times(left, right):
    return apply(left, *split(right))


def eye(rows, columns):
    shape = (rows, columns)
    return lax.broadcasted_iota(jnp.int32, shape, 0) == lax.broadcasted_iota(jnp.int32, shape, 1)


def upper_inverses(grams, base):
    spread = grams[0].shape[0]
    diagonal = eye(spread, spread)
    above = lax.broadcasted_iota(jnp.int32, (spread, spread), 0) < lax.broadcasted_iota(
        jnp.int32, (spread, spread), 1
    )
    halves = [jnp.where(diagonal, 0.5 * gram, 0.0) for gram in grams]
    columns = [jnp.sum(half, axis=0, keepdims=True) for half in halves]
    scaled = [
        jnp.where(above, gram, 0.0) / jnp.sum(half, axis=1, keepdims=True)
        for gram, half in zip(grams, halves)
    ]

    def owner(size):
        return lax.broadcasted_iota(jnp.int32, (size, spread), 1) // size

    def compact(value, size, row=lambda block: block):
        owns = owner(size)
        result = value[row(0) * size : (row(0) + 1) * size]
        for block in range(1, spread // size):
            at = row(block) * size
            result = jnp.where(owns == block, value[at : at + size], result)
        return result

    def expanded(value, size, row=lambda block: block):
        owns = owner(size)
        masks = [(owns == block).astype(BF16) for block in range(spread // size)]
        terms = []
        for term in split(value):
            rows = [jnp.zeros_like(term)] * (spread // size)
            for block, mask in enumerate(masks):
                if row(block) is not None:
                    rows[row(block)] = term * mask
            terms.append(jnp.concatenate(rows, axis=0))
        return doubled(*terms)

    size = base
    unit = compact(diagonal.astype(F32), size)
    powers = [compact(value, size) for value in scaled]
    results = [unit - power for power in powers]
    rights = [expanded(power, size) for power in powers]
    powers = [folded(dot(tall(power), right)) for power, right in zip(powers, rights)]
    reach = 2
    while reach < size:
        reach *= 2
        rights = [expanded(power, size) for power in powers]
        if reach < size:
            lefts = [jnp.concatenate([r, p], axis=0) for r, p in zip(results, powers)]
        else:
            lefts = results
        products = [folded(dot(tall(left), right)) for left, right in zip(lefts, rights)]
        results = [result + product[:size] for result, product in zip(results, products)]
        if reach < size:
            powers = [product[size:] for product in products]
    while size < spread:
        odd = lax.rem(owner(size), 2) == 1
        edges = [
            jnp.where(odd, compact(value, size, lambda block: block & ~1), 0.0) for value in scaled
        ]
        rights = [expanded(result, size) for result in results]
        products = [folded(dot(tall(edge), right)) for edge, right in zip(edges, rights)]
        rights = [
            expanded(product, size, lambda block: block - 1 if block & 1 else None)
            for product in products
        ]
        products = [folded(dot(tall(result), right)) for result, right in zip(results, rights)]
        results = [
            jnp.concatenate(
                [jnp.where(odd, -product, result), jnp.where(odd, result, 0.0)], axis=0
            )
            for result, product in zip(results, products)
        ]
        size *= 2
    return [result / column for result, column in zip(results, columns)]


def reflectors(values, active):
    double, spread = values[0].shape
    pairs = [wide(value) for value in values]
    grams = [dot(pair, pair, TN) for pair in pairs]
    grams = [
        (g[:spread, :spread] + g[spread:, spread:]) + (g[:spread, spread:] + g[spread:, :spread])
        for g in grams
    ]
    triangles = upper_inverses(grams, 16 if len(values) > 8 else 32)
    unit = eye(double, double).astype(F32)
    scaled = []
    for pair, triangle in zip(pairs, triangles):
        high, low = split(triangle)
        right = jnp.concatenate(
            [jnp.concatenate([high, high], axis=1), jnp.concatenate([low, low], axis=1)], axis=0
        )
        product = dot(pair, right, NT)
        scaled.append(product[:, :spread] + product[:, spread:])
    for pair, value, kept in zip(pairs, scaled, active):
        if kept is not True:
            value = jnp.where(kept, value, 0.0)
        yield split(unit - folded(dot(tall(value), pair, NT)))


def runs_of(slots, extra=0):
    size = next(size for size in (4, 2, 1) if slots % size == 0)
    bounds = [0, 1] + list(range(size, slots + 1, size)) if size > 1 else list(range(slots + 1))
    runs = list(zip(bounds[:-1], bounds[1:]))
    runs[-1] = (runs[-1][0], runs[-1][1] + extra)
    return runs


def edges_kernel(source, last, first):
    last[...] = source[:, source.shape[1] - 1]
    first[...] = source[0, :2]


def reflect_kernel(sweeps, last_slot, source, *refs):
    count, double, spread = source.shape[1:]
    found = [refs[i * 7 : i * 7 + 7] for i in range(len(sweeps))]
    limit = last_slot - lax.axis_index("row") * count
    values = [source[sweep, b] for sweep in sweeps for b in range(count)]
    active = [b < count - 2 or b <= limit for _ in sweeps for b in range(count)]
    for i, (high, low) in enumerate(reflectors(values, active)):
        found[i // count][0][i % count] = high
        found[i // count][1][i % count] = low
    runs = runs_of(count, 1)[1:]
    state = [[None] * len(runs) for _ in found]
    for step in range(max(stop - at for at, stop in runs)):
        for j, (at, stop) in enumerate(runs):
            if at + step >= stop:
                continue
            for i, (k_high, k_low, q_high, q_low, maps, upto, beyond) in enumerate(found):
                b = at + step - 1
                high, low = k_high[b, :spread, :], k_low[b, :spread, :]
                if step == 0:
                    both = high.astype(F32) + low.astype(F32)
                else:
                    both = apply(state[i][j], high, low)
                state[i][j] = both[:, spread:]
                q_high[b], q_low[b] = split(both[:, :spread])
                if b == count - 2 or (at + step + 1 == stop and b < count - 1):
                    maps[j] = both[:, spread:]
                if b == count - 1:
                    beyond[...] = both[:, spread:]
    so_far = [[maps[j] for j in range(len(runs))] for _, _, _, _, maps, _, _ in found]
    distance = 1
    while distance < len(runs):
        so_far = [
            each[:distance]
            + [times(each[j - distance], each[j]) for j in range(distance, len(runs))]
            for each in so_far
        ]
        distance *= 2
    for each, (_, _, _, _, _, upto, _) in zip(so_far, found):
        for j, value in enumerate(each):
            upto[j] = value


def reflect(refl_v, sweeps):
    slots, double, spread = refl_v.shape[1:]
    runs = len(runs_of(slots)) - 1
    shape = jax.ShapeDtypeStruct
    shapes = [shape((slots, double, double), BF16)] * 2
    shapes += [shape((slots, spread, spread), BF16)] * 2
    shapes += [shape((runs, spread, spread), F32)] * 2 + [shape((spread, spread), F32)]
    results = whole_call(
        functools.partial(reflect_kernel, sweeps, lax.axis_size("row") * slots - 3),
        shapes * len(sweeps), len(sweeps) * slots * 300_000_000, [], [refl_v], vmem=24,
    )
    return [results[i * 7 : i * 7 + 7] for i in range(len(sweeps))]


def edge_kernel(
    count, last_slot, left, right, upto1, upto2, beyond, left_high, left_low, right_high, right_low,
    q_high, q_low, reach, total,
):
    sweeps, _, spread = left.shape
    extra = right.shape[0]
    first = lax.axis_index("row") * count
    values = [left[i] for i in range(sweeps)] + [right[i] for i in range(extra)]
    active = [(first > 0) & (first - 1 <= last_slot)] * sweeps
    active += [first + count + i <= last_slot for i in range(extra)]
    for i, (high, low) in enumerate(reflectors(values, active)):
        if i < sweeps:
            left_high[i], left_low[i] = high, low
        else:
            right_high[i - sweeps], right_low[i - sweeps] = high, low
    state = beyond[...]
    for i in range(extra):
        both = apply(state, right_high[i, :spread, :], right_low[i, :spread, :])
        q_high[i], q_low[i] = split(both[:, :spread])
        state = both[:, spread:]
    for i, upto in enumerate((upto1, upto2)):
        entry = left_high[i, :spread, spread:].astype(F32) + left_low[i, :spread, spread:].astype(F32)
        reach[i, 0] = entry
        for j in range(upto.shape[0] - 1):
            reach[i, j + 1] = times(entry, upto[j])
        total[i] = times(entry, upto[upto.shape[0] - 1])


def merge_kernel(owners, cauchy, *refs):
    pieces, (merged, chosen) = refs[:-2], refs[-2:]
    rows, columns = pieces[0].shape
    mine = lax.axis_index("col")
    chosen[...] = rolled(cauchy[...], mine * rows)[:, : chosen.shape[1]]
    left = [
        chosen[pl.ds(pl.multiple_of((mine ^ owner) * rows, rows), rows), :rows] for owner in owners
    ]
    left_high, left_low = split(jnp.concatenate(left, axis=0))
    step = columns // 4
    for part in range(4):
        at = slice(part * step, (part + 1) * step)
        right_high, right_low = split(jnp.concatenate([piece[:, at] for piece in pieces], axis=0))
        merged[:, at] = dot(left_high, right_high, TN) + (
            dot(left_high, right_low, TN) + dot(left_low, right_high, TN)
        )


def shifted(array, by):
    devices = lax.axis_size("row")
    return lax.ppermute(array, "row", [(i, (i + by) % devices) for i in range(devices)])


def swapped(array, axis, distance):
    devices = lax.axis_size(axis)
    return lax.ppermute(array, axis, [(i, i ^ distance) for i in range(devices)])


def after_all(array, *others):
    return lax.optimization_barrier((array, *others))[0]


def rolled(value, left):
    width = value.shape[1]
    return pltpu.roll(value, lax.rem(width - left, width), 1)


def slot_table(left, own, right=None):
    (left_ref, at), extra = left, 0 if right is None else right.shape[0]
    table = [(left_ref, at)] + [(own, b) for b in range(own.shape[0])]
    return table + [(right, b) for b in range(extra)]


def chain(aligned, k_high, k_low, runs, maps, slots, y_local, joins):
    rows, spread = joins.shape[1:]
    carry = [jnp.zeros((rows, spread), F32)] * len(runs)

    def advance(j, slot):
        fresh = aligned[:, slot * spread : (slot + 1) * spread]
        (high, b), (low, _) = k_high[slot], k_low[slot]
        both = apply(jnp.concatenate([carry[j], fresh], axis=1), high[b], low[b])
        y_local[slot] = both[:, :spread]
        carry[j] = both[:, spread:]

    for step in range(max(min(stop, slots) - at for at, stop in runs)):
        for j, (at, stop) in enumerate(runs):
            if at + step < min(stop, slots):
                advance(j, at + step)
    beyond = list(range(slots, runs[-1][1]))
    joins[0] = jnp.zeros_like(carry[0])
    so_far, ends = carry[0], list(carry)
    for j in range(1, len(runs)):
        joins[j] = so_far
        so_far = times(so_far, maps[j - 1]) + ends[j]
        if beyond:
            advance(len(runs) - 1, beyond.pop(0))
    for slot in beyond:
        advance(len(runs) - 1, slot)
    return so_far


def terms(table, runs):
    return [jnp.concatenate([ref[b] for ref, b in table[at:stop]], axis=1) for at, stop in runs]


def settled(runs, joins, q_high, q_low, y_local, line):
    spread = y_local.shape[2]
    highs, lows = terms(q_high, runs[1:]), terms(q_low, runs[1:])
    for j, (at, stop) in enumerate(runs):
        added = apply(joins[j], highs[j - 1], lows[j - 1]) if j else None
        for slot in range(at, stop):
            value = y_local[slot]
            if j:
                value = value + added[:, (slot - at) * spread : (slot - at + 1) * spread]
            line[:, slot * spread : (slot + 1) * spread] = value


def reached(runs, entry, reach, q_high, q_low, line):
    spread = entry.shape[0]
    line[:, :spread] = entry
    highs, lows = terms(q_high, runs[1:]), terms(q_low, runs[1:])
    for j, (at, stop) in enumerate(runs[1:]):
        line[:, at * spread : stop * spread] = apply(reach[j], highs[j], lows[j])


def first_kernel(
    count, start, home, after, left_high, left_low, k_high, k_low, right_high, right_low, maps,
    q_high, q_low, q_right_high, q_right_low, line, state, y_local, joins,
):
    spread = state.shape[1]
    offset = start[0]
    aligned = rolled(jnp.concatenate([home[...], after[...]], axis=1), offset)
    runs = runs_of(count, y_local.shape[0] - count)
    highs = slot_table((left_high, 0), k_high, right_high)
    lows = slot_table((left_low, 0), k_low, right_low)
    state[...] = chain(aligned, highs, lows, runs, maps, count, y_local, joins)
    q_highs = slot_table((None, 0), q_high, q_right_high)
    q_lows = slot_table((None, 0), q_low, q_right_low)
    settled(runs, joins, q_highs, q_lows, y_local, line)

    @pl.when(lax.axis_index("row") == 0)
    def _():
        line[:, :spread] = pltpu.roll(home[:, :spread], lax.rem(spread - offset, spread), 1)


def second_kernel(
    count, start, line, state_in, left_high, left_low, k_high, k_low, maps, y_local, joins, state,
    head,
):
    spread = head.shape[1]
    ahead = start[1] - start[0]
    aligned = rolled(line[...], ahead + spread)
    runs = runs_of(count, y_local.shape[0] - count)
    highs, lows = slot_table((left_high, 1), k_high), slot_table((left_low, 1), k_low)
    state[:, spread:] = chain(aligned, highs, lows, runs, maps, count, y_local, joins)
    state[:, :spread] = state_in[...]
    head[...] = pltpu.roll(
        line[:, : 2 * spread], lax.rem(4 * spread - ahead, 2 * spread), 1
    )[:, :spread]


def base_kernel(count, start, head, joins, y_local, q_high, q_low, base, line):
    spread = head.shape[1]
    runs = runs_of(count, y_local.shape[0] - count)
    q_highs, q_lows = slot_table((None, 0), q_high), slot_table((None, 0), q_low)
    settled(runs, joins, q_highs, q_lows, y_local, line)

    @pl.when(lax.axis_index("row") == 0)
    def _():
        line[:, :spread] = head[...]

    base[...] = rolled(line[...], spread - start[1])[:, : base.shape[1]]


def response_kernel(
    count, start, q_high, q_low, q_right_high, q_right_low, reach, left_high, left_low, k_high,
    k_low, maps, totals, y_local, joins, through_device, line,
):
    spread = line.shape[0]
    entry = left_high[0, :spread, :spread].astype(F32) + left_low[0, :spread, :spread].astype(F32)
    q_highs = slot_table((None, 0), q_high, q_right_high)
    q_lows = slot_table((None, 0), q_low, q_right_low)
    reached(runs_of(count, line.shape[1] // spread - count), entry, reach.at[0], q_highs, q_lows, line)
    aligned = rolled(line[...], start[1] - start[0] + spread)
    runs = runs_of(count, y_local.shape[0] - count)
    highs, lows = slot_table((left_high, 1), k_high), slot_table((left_low, 1), k_low)
    through_device[1] = chain(aligned, highs, lows, runs, maps, count, y_local, joins)
    through_device[0], through_device[2] = totals[0], totals[1]


def home_kernel(
    count, start, joins, y_local, q_high, q_low, reach, left_high, left_low, high, low, line
):
    spread, columns = line.shape[0], high.shape[1]
    runs = runs_of(count, y_local.shape[0] - count)
    q_highs, q_lows = slot_table((None, 0), q_high), slot_table((None, 0), q_low)
    for sweep in range(2):
        at = slice(sweep * spread, (sweep + 1) * spread)
        if sweep == 0:
            settled(runs, joins, q_highs, q_lows, y_local, line)
        else:
            entry = left_high[1, :spread, :spread].astype(F32)
            entry = entry + left_low[1, :spread, :spread].astype(F32)
            reached(runs, entry, reach.at[1], q_highs, q_lows, line)
        high[at], low[at] = split(rolled(line[...], spread - start[1])[:, :columns])


def is_upper(level):
    return lax.rem(lax.axis_index("row") // (1 << level), 2) == 1


def through(states, maps):
    spread = maps.shape[1]
    first, second = states[:, :spread], states[:, spread:]
    return jnp.concatenate(
        [times(first, maps[0]), times(first, maps[1]) + times(second, maps[2])], axis=1
    )


def join_maps_kernel(level, *refs):
    upper = is_upper(level)
    mine, other, (high, both, inside) = refs[0], refs[1], refs[-3:]
    inner = refs[2]
    spread = both.shape[1]
    low = [jnp.where(upper, other[i], mine[i]) for i in range(3)]
    for i in range(3):
        high[i] = jnp.where(upper, mine[i], other[i])

    def joined(later):
        return [
            times(low[0], later[0]),
            times(low[0], later[1]) + times(low[1], later[2]),
            times(low[2], later[2]),
        ]

    for i, value in enumerate(joined(high)):
        both[i] = value
    if level:
        for i, value in enumerate(joined(inner)):
            inside[i] = jnp.where(upper, value, inner[i])
    else:
        unit = eye(spread, spread).astype(F32)
        for i, value in enumerate([unit, jnp.zeros_like(unit), unit]):
            inside[i] = jnp.where(upper, low[i], value)


def join_states_kernel(level, mine, other, high, *refs):
    upper = is_upper(level)
    if level:
        inner, before, refs = refs[0], refs[1], refs[2:]
    low = jnp.where(upper, other[...], mine[...])
    refs[0][...] = through(low, high) + jnp.where(upper, mine[...], other[...])
    if level:
        refs[1][...] = before[...] + jnp.where(upper, through(low, inner), 0.0)
    else:
        refs[1][...] = jnp.where(upper, low, 0.0)


def final_kernel(levels, half, inner, before, base, high, low, out):
    enters = jnp.where(is_upper(levels - 1), half[...], 0.0)
    incoming = before[...] + through(enters, inner)
    out[...] = base[...] + apply(incoming, high[...], low[...])


def whole_call(kernel, shapes, flops, scalars, arrays, scratch=(), vmem=8):
    return pl.pallas_call(
        kernel,
        out_shape=shapes,
        in_specs=[SMEM] * len(scalars) + [VMEM] * len(arrays),
        out_specs=jax.tree.map(lambda shape: VMEM, shapes),
        scratch_shapes=list(scratch),
        compiler_params=pltpu.CompilerParams(vmem_limit_bytes=vmem << 20),
        cost_estimate=pl.CostEstimate(
            flops=flops, bytes_accessed=4_000_000, transcendentals=0
        ),
    )(*scalars, *arrays)


def shards(panel, cauchy, refl_v, block_start):
    rows, columns = panel.shape
    slots, _, spread = refl_v.shape[1:]
    levels = lax.axis_size("row").bit_length() - 1
    last_slot = lax.axis_size("row") * slots - 3
    shape = functools.partial(jax.ShapeDtypeStruct, dtype=F32)
    starts = [block_start]
    count, runs = lax.axis_size("col"), len(runs_of(slots))
    square = (spread, spread)

    pieces, owners = [panel], [0]
    distance = count // 2
    while distance:
        pieces += [swapped(piece, "col", distance) for piece in pieces]
        if owners == [0]:
            pair = shape((2,) + refl_v.shape[2:])
            left, right = whole_call(edges_kernel, [pair, pair], 10_000_000, [], [refl_v])
            left, right = shifted(left, 1), shifted(right, -1)
            if slots <= 16:
                one, two = reflect(refl_v, (0, 1))
            else:
                [one], [two] = reflect(refl_v, (0,)), reflect(refl_v, (1,))
            high1, low1, qh1, ql1, maps1, upto1, beyond = one
            high2, low2, qh2, ql2, maps2, upto2, _ = two
            pieces[-1] = after_all(pieces[-1], beyond, left, right)
        owners += [owner ^ distance for owner in owners]
        distance //= 2
    k_pair = jax.ShapeDtypeStruct((2,) + (2 * spread, 2 * spread), BF16)
    q_pair = jax.ShapeDtypeStruct((2,) + square, BF16)
    lh, ll, rh, rl, qrh, qrl, reach, totals = whole_call(
        functools.partial(edge_kernel, slots, last_slot),
        [k_pair] * 4 + [q_pair] * 2 + [shape((2, runs - 1) + square), shape((2,) + square)],
        2_000_000_000, [], [left, right, upto1, upto2, beyond],
    )
    pieces[0] = after_all(pieces[0], totals)
    merged = whole_call(
        functools.partial(merge_kernel, owners), shape((rows, columns)),
        1_000_000_000, [], [cauchy] + pieces,
        [pltpu.VMEM((cauchy.shape[0], 128 * pl.cdiv(rows, 128)), F32)],
    )
    after = shifted(merged[:, : 4 * spread], -1)

    y_response, joins_response, maps = whole_call(
        functools.partial(response_kernel, slots),
        [shape((slots + 1,) + square), shape((runs,) + square), shape((3,) + square)],
        4_000_000_000, starts,
        [qh1, ql1, qrh, qrl, after_all(reach, merged), lh, ll, high2, low2, maps2,
         totals],
        [pltpu.VMEM((spread, columns + 3 * spread), F32)],
    )
    line, state1 = whole_call(
        functools.partial(first_kernel, slots),
        [shape((rows, columns + 3 * spread)), shape((rows, spread))], 3_000_000_000, starts,
        [after_all(merged, maps), after, lh, ll, high1, low1, rh, rl, maps1, qh1, ql1, qrh, qrl],
        [pltpu.VMEM((slots + 3, rows, spread), F32), pltpu.VMEM((runs, rows, spread), F32)],
    )
    states = shape((rows, 2 * spread))
    y2, joins2, state, head2 = whole_call(
        functools.partial(second_kernel, slots),
        [shape((slots + 1, rows, spread)), shape((runs, rows, spread)), states,
         shape((rows, spread))],
        3_000_000_000, starts,
        [line, state1, lh, ll, high2, low2, maps2],
    )
    groups = []
    for level in range(levels - 1):
        other = swapped(maps, "row", 1 << level)
        arrays = [maps, other if level else after_all(other, state)]
        arrays += [inside] if level else []
        high, maps, inside = whole_call(
            functools.partial(join_maps_kernel, level), [shape((3,) + square)] * 3,
            400_000_000, [], arrays,
        )
        groups.append((high, inside))

    base = whole_call(
        functools.partial(base_kernel, slots), shape((rows, columns)), 2_000_000_000, starts,
        [head2, joins2, y2, qh2, ql2], [pltpu.VMEM((rows, columns + spread), F32)],
    )
    enters = None
    for level in range(levels - 1):
        arrays = [state, swapped(state, "row", 1 << level), groups[level][0]]
        arrays += [groups[level - 1][1], enters] if level else []
        state, enters = whole_call(
            functools.partial(join_states_kernel, level), [states] * 2, 100_000_000, [], arrays,
        )
    half = swapped(state, "row", 1 << (levels - 1))
    home = jax.ShapeDtypeStruct((2 * spread, columns), BF16)
    home_high, home_low = whole_call(
        functools.partial(home_kernel, slots), [home, home], 3_000_000_000, starts,
        [after_all(joins_response, state), y_response, qh2, ql2, reach, lh, ll],
        [pltpu.VMEM((spread, columns + spread), F32)],
    )
    return whole_call(
        functools.partial(final_kernel, levels), shape((rows, columns)), 1_000_000_000, [],
        [half, groups[-1][1], enters, base, home_high, home_low],
    )


def solution(mesh):
    placed = (P("col", "row"), P(), P(None, "row", None, None), P())
    return jax.shard_map(
        shards, mesh=mesh, in_specs=placed, out_specs=P("col", "row"), check_vma=False
    )
```

```python
import functools

import jax
import jax.numpy as jnp
from jax import lax
from jax.experimental import pallas as pl
from jax.experimental.pallas import tpu as pltpu
from jax.sharding import PartitionSpec as P

F32, BF16 = jnp.float32, jnp.bfloat16
VMEM = pl.BlockSpec(memory_space=pltpu.VMEM)
SMEM = pl.BlockSpec(memory_space=pltpu.SMEM)
NN = (((1,), (0,)), ((), ()))
NT = (((1,), (1,)), ((), ()))
TN = (((0,), (0,)), ((), ()))


def split(value):
    high = value.astype(BF16)
    return high, (value - high.astype(F32)).astype(BF16)


def dot(left, right, dims=NN):
    return lax.dot_general(left, right, dims, preferred_element_type=F32)


def wide(value):
    return jnp.concatenate(split(value), axis=1)


def tall(value):
    terms = [jnp.concatenate([term, term], axis=1) for term in split(value)]
    return jnp.concatenate(terms, axis=0)


def doubled(rows_high, rows_low):
    return jnp.concatenate([rows_high, rows_low], axis=0)


def folded(product):
    half = product.shape[0] // 2
    return product[:half] + product[half:]


def apply(left, high, low):
    if left.shape[1] <= 128:
        return folded(dot(tall(left), doubled(high, low)))
    left_high, left_low = split(left)
    return folded(dot(jnp.concatenate([left_high, left_low], axis=0), high)) + dot(left_high, low)


def times(left, right):
    return apply(left, *split(right))


def eye(rows, columns):
    shape = (rows, columns)
    return lax.broadcasted_iota(jnp.int32, shape, 0) == lax.broadcasted_iota(jnp.int32, shape, 1)


def upper_inverses(grams, base):
    spread = grams[0].shape[0]
    diagonal = eye(spread, spread)
    above = lax.broadcasted_iota(jnp.int32, (spread, spread), 0) < lax.broadcasted_iota(
        jnp.int32, (spread, spread), 1
    )
    halves = [jnp.where(diagonal, 0.5 * gram, 0.0) for gram in grams]
    columns = [jnp.sum(half, axis=0, keepdims=True) for half in halves]
    scaled = [
        jnp.where(above, gram, 0.0) / jnp.sum(half, axis=1, keepdims=True)
        for gram, half in zip(grams, halves)
    ]

    def owner(size):
        return lax.broadcasted_iota(jnp.int32, (size, spread), 1) // size

    def compact(value, size, row=lambda block: block):
        owns = owner(size)
        result = value[row(0) * size : (row(0) + 1) * size]
        for block in range(1, spread // size):
            at = row(block) * size
            result = jnp.where(owns == block, value[at : at + size], result)
        return result

    def expanded(value, size, row=lambda block: block):
        owns = owner(size)
        masks = [(owns == block).astype(BF16) for block in range(spread // size)]
        terms = []
        for term in split(value):
            rows = [jnp.zeros_like(term)] * (spread // size)
            for block, mask in enumerate(masks):
                if row(block) is not None:
                    rows[row(block)] = term * mask
            terms.append(jnp.concatenate(rows, axis=0))
        return doubled(*terms)

    size = base
    unit = compact(diagonal.astype(F32), size)
    powers = [compact(value, size) for value in scaled]
    results = [unit - power for power in powers]
    rights = [expanded(power, size) for power in powers]
    powers = [folded(dot(tall(power), right)) for power, right in zip(powers, rights)]
    reach = 2
    while reach < size:
        reach *= 2
        rights = [expanded(power, size) for power in powers]
        if reach < size:
            lefts = [jnp.concatenate([r, p], axis=0) for r, p in zip(results, powers)]
        else:
            lefts = results
        products = [folded(dot(tall(left), right)) for left, right in zip(lefts, rights)]
        results = [result + product[:size] for result, product in zip(results, products)]
        if reach < size:
            powers = [product[size:] for product in products]
    while size < spread:
        odd = lax.rem(owner(size), 2) == 1
        edges = [
            jnp.where(odd, compact(value, size, lambda block: block & ~1), 0.0) for value in scaled
        ]
        rights = [expanded(result, size) for result in results]
        products = [folded(dot(tall(edge), right)) for edge, right in zip(edges, rights)]
        rights = [
            expanded(product, size, lambda block: block - 1 if block & 1 else None)
            for product in products
        ]
        products = [folded(dot(tall(result), right)) for result, right in zip(results, rights)]
        results = [
            jnp.concatenate(
                [jnp.where(odd, -product, result), jnp.where(odd, result, 0.0)], axis=0
            )
            for result, product in zip(results, products)
        ]
        size *= 2
    return [result / column for result, column in zip(results, columns)]


def reflectors(values, active):
    double, spread = values[0].shape
    pairs = [wide(value) for value in values]
    grams = [dot(pair, pair, TN) for pair in pairs]
    grams = [
        (g[:spread, :spread] + g[spread:, spread:]) + (g[:spread, spread:] + g[spread:, :spread])
        for g in grams
    ]
    triangles = upper_inverses(grams, 16 if len(values) > 8 else 32)
    unit = eye(double, double).astype(F32)
    scaled = []
    for pair, triangle in zip(pairs, triangles):
        high, low = split(triangle)
        right = jnp.concatenate(
            [jnp.concatenate([high, high], axis=1), jnp.concatenate([low, low], axis=1)], axis=0
        )
        product = dot(pair, right, NT)
        scaled.append(product[:, :spread] + product[:, spread:])
    for pair, value, kept in zip(pairs, scaled, active):
        if kept is not True:
            value = jnp.where(kept, value, 0.0)
        yield split(unit - folded(dot(tall(value), pair, NT)))


def runs_of(slots, extra=0):
    size = next(size for size in (4, 2, 1) if slots % size == 0)
    bounds = [0, 1] + list(range(size, slots + 1, size)) if size > 1 else list(range(slots + 1))
    runs = list(zip(bounds[:-1], bounds[1:]))
    runs[-1] = (runs[-1][0], runs[-1][1] + extra)
    return runs


def edges_kernel(source, kept, last, first):
    last[...] = source[:, source.shape[1] - 1]
    first[...] = source[0, :2]


def reflect_kernel(sweeps, last_slot, source, *refs):
    count, double, spread = source.shape[1:]
    found = [refs[i * 8 : i * 8 + 8] for i in range(len(sweeps))]
    limit = last_slot - lax.axis_index("row") * count
    values = [source[sweep, b] for sweep in sweeps for b in range(count)]
    active = [b < count - 2 or b <= limit for _ in sweeps for b in range(count)]
    for i, (high, low) in enumerate(reflectors(values, active)):
        found[i // count][0][i % count] = high
        found[i // count][1][i % count] = low
    runs = runs_of(count, 1)[1:]
    state = [[None] * len(runs) for _ in found]
    maps = [[None] * len(runs) for _ in found]
    for step in range(max(stop - at for at, stop in runs)):
        for j, (at, stop) in enumerate(runs):
            if at + step >= stop:
                continue
            for i, (k_high, k_low, q_high, q_low, _, _, _, beyond) in enumerate(found):
                b = at + step - 1
                high, low = k_high[b, :spread, :], k_low[b, :spread, :]
                if step == 0:
                    both = high.astype(F32) + low.astype(F32)
                else:
                    both = apply(state[i][j], high, low)
                state[i][j] = both[:, spread:]
                q_high[b], q_low[b] = split(both[:, :spread])
                if b == count - 2 or (at + step + 1 == stop and b < count - 1):
                    maps[i][j] = both[:, spread:]
                if b == count - 1:
                    beyond[...] = both[:, spread:]
    for each, (_, _, _, _, join_high, join_low, upto, _) in zip(maps, found):
        spans = {(j, j + 1): value for j, value in enumerate(each)}
        length = 2
        while length <= len(runs):
            half = 1 << ((length - 1).bit_length() - 1)
            for j in range(len(runs) - length + 1):
                spans[j, j + length] = times(spans[j, j + half], spans[j + half, j + length])
            length += 1
        for j in range(len(runs)):
            upto[j] = spans[0, j + 1]
            for stop in range(len(runs)):
                block = spans.get((j, stop + 1), jnp.zeros((spread, spread), F32))
                rows, columns = (slice(i * spread, (i + 1) * spread) for i in (j, stop))
                join_high[rows, columns], join_low[rows, columns] = split(block)


def reflect(refl_v, sweeps):
    slots, double, spread = refl_v.shape[1:]
    runs = len(runs_of(slots)) - 1
    shape = jax.ShapeDtypeStruct
    shapes = [shape((slots, double, double), BF16)] * 2
    shapes += [shape((slots, spread, spread), BF16)] * 2
    shapes += [shape((runs * spread, runs * spread), BF16)] * 2
    shapes += [shape((runs, spread, spread), F32), shape((spread, spread), F32)]
    results = whole_call(
        functools.partial(reflect_kernel, sweeps, lax.axis_size("row") * slots - 3),
        shapes * len(sweeps), len(sweeps) * slots * 300_000_000, [], [refl_v], vmem=24,
    )
    return [results[i * 8 : i * 8 + 8] for i in range(len(sweeps))]


def edge_kernel(
    count, last_slot, left, right, upto1, upto2, beyond, left_high, left_low, right_high, right_low,
    q_high, q_low, reach, total,
):
    sweeps, _, spread = left.shape
    extra = right.shape[0]
    first = lax.axis_index("row") * count
    values = [left[i] for i in range(sweeps)] + [right[i] for i in range(extra)]
    active = [(first > 0) & (first - 1 <= last_slot)] * sweeps
    active += [first + count + i <= last_slot for i in range(extra)]
    for i, (high, low) in enumerate(reflectors(values, active)):
        if i < sweeps:
            left_high[i], left_low[i] = high, low
        else:
            right_high[i - sweeps], right_low[i - sweeps] = high, low
    state = beyond[...]
    for i in range(extra):
        both = apply(state, right_high[i, :spread, :], right_low[i, :spread, :])
        q_high[i], q_low[i] = split(both[:, :spread])
        state = both[:, spread:]
    for i, upto in enumerate((upto1, upto2)):
        entry = left_high[i, :spread, spread:].astype(F32) + left_low[i, :spread, spread:].astype(F32)
        reach[i, 0] = entry
        for j in range(upto.shape[0] - 1):
            reach[i, j + 1] = times(entry, upto[j])
        total[i] = times(entry, upto[upto.shape[0] - 1])


def merge_kernel(owners, cauchy, *refs):
    pieces, (merged, chosen) = refs[:-2], refs[-2:]
    rows, columns = pieces[0].shape
    mine = lax.axis_index("col")
    chosen[...] = rolled(cauchy[...], mine * rows)[:, : chosen.shape[1]]
    left = [
        chosen[pl.ds(pl.multiple_of((mine ^ owner) * rows, rows), rows), :rows] for owner in owners
    ]
    left_high, left_low = split(jnp.concatenate(left, axis=0))
    step = columns // 4
    for part in range(4):
        at = slice(part * step, (part + 1) * step)
        right_high, right_low = split(jnp.concatenate([piece[:, at] for piece in pieces], axis=0))
        merged[:, at] = dot(left_high, right_high, TN) + (
            dot(left_high, right_low, TN) + dot(left_low, right_high, TN)
        )


def shifted(array, by):
    devices = lax.axis_size("row")
    return lax.ppermute(array, "row", [(i, (i + by) % devices) for i in range(devices)])


def swapped(array, axis, distance):
    devices = lax.axis_size(axis)
    return lax.ppermute(array, axis, [(i, i ^ distance) for i in range(devices)])


def after_all(array, *others):
    return lax.optimization_barrier((array, *others))[0]


def rolled(value, left):
    width = value.shape[1]
    return pltpu.roll(value, lax.rem(width - left, width), 1)


def slot_table(left, own, right=None):
    (left_ref, at), extra = left, 0 if right is None else right.shape[0]
    table = [(left_ref, at)] + [(own, b) for b in range(own.shape[0])]
    return table + [(right, b) for b in range(extra)]


def chain(aligned, k_high, k_low, runs, join_high, join_low, slots, y_local, joins):
    rows, spread = joins.shape[1:]
    carry = [jnp.zeros((rows, spread), F32)] * len(runs)

    def advance(j, slot):
        fresh = aligned[:, slot * spread : (slot + 1) * spread]
        (high, b), (low, _) = k_high[slot], k_low[slot]
        both = apply(jnp.concatenate([carry[j], fresh], axis=1), high[b], low[b])
        y_local[slot] = both[:, :spread]
        carry[j] = both[:, spread:]

    for step in range(max(min(stop, slots) - at for at, stop in runs)):
        for j, (at, stop) in enumerate(runs):
            if at + step < min(stop, slots):
                advance(j, at + step)
    beyond = list(range(slots, runs[-1][1]))
    added = apply(jnp.concatenate(carry[:-1], axis=1), join_high[...], join_low[...])
    joins[0], joins[1] = jnp.zeros_like(carry[0]), carry[0]
    entered = [added[:, j * spread : (j + 1) * spread] + carry[j + 1] for j in range(len(runs) - 1)]
    for j, value in enumerate(entered[:-1]):
        joins[j + 2] = value
    for slot in beyond:
        advance(len(runs) - 1, slot)
    return entered[-1]


def terms(table, runs):
    return [jnp.concatenate([ref[b] for ref, b in table[at:stop]], axis=1) for at, stop in runs]


def settled(runs, joins, q_high, q_low, y_local, line):
    spread = y_local.shape[2]
    highs, lows = terms(q_high, runs[1:]), terms(q_low, runs[1:])
    for j, (at, stop) in enumerate(runs):
        added = apply(joins[j], highs[j - 1], lows[j - 1]) if j else None
        for slot in range(at, stop):
            value = y_local[slot]
            if j:
                value = value + added[:, (slot - at) * spread : (slot - at + 1) * spread]
            line[:, slot * spread : (slot + 1) * spread] = value


def reached(runs, entry, reach, q_high, q_low, line):
    spread = entry.shape[0]
    line[:, :spread] = entry
    highs, lows = terms(q_high, runs[1:]), terms(q_low, runs[1:])
    for j, (at, stop) in enumerate(runs[1:]):
        line[:, at * spread : stop * spread] = apply(reach[j], highs[j], lows[j])


def first_kernel(
    count, start, home, after, left_high, left_low, k_high, k_low, right_high, right_low, join_high,
    join_low, q_high, q_low, q_right_high, q_right_low, line, state, y_local, joins,
):
    spread = state.shape[1]
    offset = start[0]
    aligned = rolled(jnp.concatenate([home[...], after[...]], axis=1), offset)
    runs = runs_of(count, y_local.shape[0] - count)
    highs = slot_table((left_high, 0), k_high, right_high)
    lows = slot_table((left_low, 0), k_low, right_low)
    state[...] = chain(aligned, highs, lows, runs, join_high, join_low, count, y_local, joins)
    q_highs = slot_table((None, 0), q_high, q_right_high)
    q_lows = slot_table((None, 0), q_low, q_right_low)
    settled(runs, joins, q_highs, q_lows, y_local, line)

    @pl.when(lax.axis_index("row") == 0)
    def _():
        line[:, :spread] = pltpu.roll(home[:, :spread], lax.rem(spread - offset, spread), 1)


def second_kernel(
    count, start, line, state_in, left_high, left_low, k_high, k_low, join_high, join_low, y_local,
    joins, state, head,
):
    spread = head.shape[1]
    ahead = start[1] - start[0]
    aligned = rolled(line[...], ahead + spread)
    runs = runs_of(count, y_local.shape[0] - count)
    highs, lows = slot_table((left_high, 1), k_high), slot_table((left_low, 1), k_low)
    state[:, spread:] = chain(
        aligned, highs, lows, runs, join_high, join_low, count, y_local, joins
    )
    state[:, :spread] = state_in[...]
    head[...] = pltpu.roll(
        line[:, : 2 * spread], lax.rem(4 * spread - ahead, 2 * spread), 1
    )[:, :spread]


def base_kernel(count, start, head, joins, y_local, q_high, q_low, base, line):
    spread = head.shape[1]
    runs = runs_of(count, y_local.shape[0] - count)
    q_highs, q_lows = slot_table((None, 0), q_high), slot_table((None, 0), q_low)
    settled(runs, joins, q_highs, q_lows, y_local, line)

    @pl.when(lax.axis_index("row") == 0)
    def _():
        line[:, :spread] = head[...]

    base[...] = rolled(line[...], spread - start[1])[:, : base.shape[1]]


def response_kernel(
    count, start, q_high, q_low, q_right_high, q_right_low, reach, left_high, left_low, k_high,
    k_low, join_high, join_low, totals, y_local, joins, through_device, line,
):
    spread = line.shape[0]
    entry = left_high[0, :spread, :spread].astype(F32) + left_low[0, :spread, :spread].astype(F32)
    q_highs = slot_table((None, 0), q_high, q_right_high)
    q_lows = slot_table((None, 0), q_low, q_right_low)
    reached(runs_of(count, line.shape[1] // spread - count), entry, reach.at[0], q_highs, q_lows, line)
    aligned = rolled(line[...], start[1] - start[0] + spread)
    runs = runs_of(count, y_local.shape[0] - count)
    highs, lows = slot_table((left_high, 1), k_high), slot_table((left_low, 1), k_low)
    through_device[1] = chain(
        aligned, highs, lows, runs, join_high, join_low, count, y_local, joins
    )
    through_device[0], through_device[2] = totals[0], totals[1]


def moved_home(start, line, high, low):
    spread, columns = high.shape
    high[...], low[...] = split(rolled(line[...], spread - start[1])[:, :columns])


def home_first_kernel(count, start, joins, y_local, q_high, q_low, high, low, line):
    runs = runs_of(count, y_local.shape[0] - count)
    q_highs, q_lows = slot_table((None, 0), q_high), slot_table((None, 0), q_low)
    settled(runs, joins, q_highs, q_lows, y_local, line)
    moved_home(start, line, high, low)


def home_second_kernel(count, start, reach, q_high, q_low, left_high, left_low, high, low, line):
    spread = line.shape[0]
    entry = left_high[1, :spread, :spread].astype(F32) + left_low[1, :spread, :spread].astype(F32)
    q_highs, q_lows = slot_table((None, 0), q_high), slot_table((None, 0), q_low)
    reached(runs_of(count, 1), entry, reach.at[1], q_highs, q_lows, line)
    moved_home(start, line, high, low)


def is_upper(level):
    return lax.rem(lax.axis_index("row") // (1 << level), 2) == 1


def through(states, maps):
    spread = maps.shape[1]
    first, second = states[:, :spread], states[:, spread:]
    return jnp.concatenate(
        [times(first, maps[0]), times(first, maps[1]) + times(second, maps[2])], axis=1
    )


def join_maps_kernel(level, *refs):
    upper = is_upper(level)
    mine, other, refs = refs[0], refs[1], list(refs[2:])
    inner = refs.pop(0) if level else None
    high, inside, *both = refs
    spread = high.shape[1]
    low = [jnp.where(upper, other[i], mine[i]) for i in range(3)]
    for i in range(3):
        high[i] = jnp.where(upper, mine[i], other[i])

    def joined(later):
        return [
            times(low[0], later[0]),
            times(low[0], later[1]) + times(low[1], later[2]),
            times(low[2], later[2]),
        ]

    if both:
        for i, value in enumerate(joined(high)):
            both[0][i] = value
    if level:
        for i, value in enumerate(joined(inner)):
            inside[i] = jnp.where(upper, value, inner[i])
    else:
        unit = eye(spread, spread).astype(F32)
        for i, value in enumerate([unit, jnp.zeros_like(unit), unit]):
            inside[i] = jnp.where(upper, low[i], value)


def join_states_kernel(level, mine, other, high, *refs):
    upper = is_upper(level)
    if level:
        inner, before, refs = refs[0], refs[1], refs[2:]
    low = jnp.where(upper, other[...], mine[...])
    refs[0][...] = through(low, high) + jnp.where(upper, mine[...], other[...])
    if level:
        refs[1][...] = before[...] + jnp.where(upper, through(low, inner), 0.0)
    else:
        refs[1][...] = jnp.where(upper, low, 0.0)


def final_kernel(
    levels, half, inner, before, base, high_first, high_second, low_first, low_second, out
):
    enters = jnp.where(is_upper(levels - 1), half[...], 0.0)
    incoming = before[...] + through(enters, inner)
    high = jnp.concatenate([high_first[...], high_second[...]], axis=0)
    low = jnp.concatenate([low_first[...], low_second[...]], axis=0)
    out[...] = base[...] + apply(incoming, high, low)


def whole_call(kernel, shapes, flops, scalars, arrays, scratch=(), vmem=8, aliases={}):
    return pl.pallas_call(
        kernel,
        out_shape=shapes,
        in_specs=[SMEM] * len(scalars) + [VMEM] * len(arrays),
        out_specs=jax.tree.map(lambda shape: VMEM, shapes),
        scratch_shapes=list(scratch),
        input_output_aliases=aliases,
        compiler_params=pltpu.CompilerParams(vmem_limit_bytes=vmem << 20),
        cost_estimate=pl.CostEstimate(
            flops=flops, bytes_accessed=4_000_000, transcendentals=0
        ),
    )(*scalars, *arrays)


def shards(panel, cauchy, refl_v, block_start):
    rows, columns = panel.shape
    slots, _, spread = refl_v.shape[1:]
    levels = lax.axis_size("row").bit_length() - 1
    last_slot = lax.axis_size("row") * slots - 3
    shape = functools.partial(jax.ShapeDtypeStruct, dtype=F32)
    starts = [block_start]
    count, runs = lax.axis_size("col"), len(runs_of(slots))
    square = (spread, spread)

    pieces, owners = [panel], [0]
    distance = count // 2
    while distance:
        pieces += [swapped(piece, "col", distance) for piece in pieces]
        if owners == [0]:
            pair = shape((2,) + refl_v.shape[2:])
            refl_v, left, right = whole_call(
                edges_kernel, [shape(refl_v.shape), pair, pair], 10_000_000, [], [refl_v],
                aliases={0: 0},
            )
            left, right = shifted(left, 1), shifted(right, -1)
            if slots <= 16:
                one, two = reflect(refl_v, (0, 1))
            else:
                [one], [two] = reflect(refl_v, (0,)), reflect(refl_v, (1,))
            high1, low1, qh1, ql1, *joins1, upto1, beyond = one
            high2, low2, qh2, ql2, *joins2, upto2, _ = two
            pieces = list(lax.optimization_barrier((*pieces, beyond, left, right))[:2])
        owners += [owner ^ distance for owner in owners]
        distance //= 2
    k_pair = jax.ShapeDtypeStruct((2,) + (2 * spread, 2 * spread), BF16)
    q_pair = jax.ShapeDtypeStruct((2,) + square, BF16)
    lh, ll, rh, rl, qrh, qrl, reach, totals = whole_call(
        functools.partial(edge_kernel, slots, last_slot),
        [k_pair] * 4 + [q_pair] * 2 + [shape((2, runs - 1) + square), shape((2,) + square)],
        2_000_000_000, [], [left, right, upto1, upto2, beyond],
    )
    pieces[0] = after_all(pieces[0], totals)
    merged = whole_call(
        functools.partial(merge_kernel, owners), shape((rows, columns)),
        1_000_000_000, [], [cauchy] + pieces,
        [pltpu.VMEM((cauchy.shape[0], 128 * pl.cdiv(rows, 128)), F32)],
    )
    after = shifted(merged[:, : 4 * spread], -1)

    y_response, joins_response, maps = whole_call(
        functools.partial(response_kernel, slots),
        [shape((slots + 1,) + square), shape((runs,) + square), shape((3,) + square)],
        4_000_000_000, starts,
        [qh1, ql1, qrh, qrl, after_all(reach, merged), lh, ll, high2, low2, *joins2,
         totals],
        [pltpu.VMEM((spread, columns + 3 * spread), F32)],
    )
    line, state1 = whole_call(
        functools.partial(first_kernel, slots),
        [shape((rows, columns + 3 * spread)), shape((rows, spread))], 3_000_000_000, starts,
        [after_all(merged, maps), after, lh, ll, high1, low1, rh, rl, *joins1, qh1, ql1, qrh, qrl],
        [pltpu.VMEM((slots + 3, rows, spread), F32), pltpu.VMEM((runs, rows, spread), F32)],
    )
    states = shape((rows, 2 * spread))
    y2, entries2, state, head2 = whole_call(
        functools.partial(second_kernel, slots),
        [shape((slots + 1, rows, spread)), shape((runs, rows, spread)), states,
         shape((rows, spread))],
        3_000_000_000, starts,
        [line, state1, lh, ll, high2, low2, *joins2],
    )
    home = jax.ShapeDtypeStruct((spread, columns), BF16)
    home_line = pltpu.VMEM((spread, columns + spread), F32)
    high_second, low_second = whole_call(
        functools.partial(home_second_kernel, slots), [home, home], 3_000_000_000, starts,
        [after_all(reach, state), qh2, ql2, lh, ll], [home_line],
    )
    groups, inside, enters = [], None, None
    for level in range(levels - 1):
        other, state_other = swapped(maps, "row", 1 << level), swapped(state, "row", 1 << level)
        if level == 0:
            other = after_all(other, state)
        if level == levels - 2:
            base = whole_call(
                functools.partial(base_kernel, slots), shape((rows, columns)), 2_000_000_000, starts,
                [after_all(head2, state), entries2, y2, qh2, ql2],
                [pltpu.VMEM((rows, columns + spread), F32)],
            )
            other = after_all(other, base)
        high, inner, *maps = whole_call(
            functools.partial(join_maps_kernel, level),
            [shape((3,) + square)] * (2 if level == levels - 2 else 3), 400_000_000, [],
            [maps, other] + ([inside] if level else []),
        )
        maps = maps[0] if maps else None
        arrays = [state, state_other, high] + ([inside, enters] if level else [])
        state, enters = whole_call(
            functools.partial(join_states_kernel, level), [states] * 2, 100_000_000, [], arrays,
        )
        inside = inner
    half = swapped(state, "row", 1 << (levels - 1))
    high_first, low_first = whole_call(
        functools.partial(home_first_kernel, slots), [home, home], 1_500_000_000, starts,
        [after_all(joins_response, state), y_response, qh2, ql2], [home_line],
    )
    return whole_call(
        functools.partial(final_kernel, levels), shape((rows, columns)), 1_000_000_000, [],
        [half, inside, enters, base, high_first, high_second, low_first, low_second],
    )


def solution(mesh):
    placed = (P("col", "row"), P(), P(None, "row", None, None), P())
    return jax.shard_map(
        shards, mesh=mesh, in_specs=placed, out_specs=P("col", "row"), check_vma=False
    )
```

```python
import functools

import jax
import jax.numpy as jnp
from jax import lax
from jax.experimental import pallas as pl
from jax.experimental.pallas import tpu as pltpu
from jax.sharding import PartitionSpec as P

F32, BF16 = jnp.float32, jnp.bfloat16
VMEM = pl.BlockSpec(memory_space=pltpu.VMEM)
SMEM = pl.BlockSpec(memory_space=pltpu.SMEM)
NN = (((1,), (0,)), ((), ()))
NT = (((1,), (1,)), ((), ()))
TN = (((0,), (0,)), ((), ()))


def split(value):
    high = value.astype(BF16)
    return high, (value - high.astype(F32)).astype(BF16)


def dot(left, right, dims=NN):
    return lax.dot_general(left, right, dims, preferred_element_type=F32)


def wide(value):
    return jnp.concatenate(split(value), axis=1)


def tall(value):
    terms = [jnp.concatenate([term, term], axis=1) for term in split(value)]
    return jnp.concatenate(terms, axis=0)


def doubled(rows_high, rows_low):
    return jnp.concatenate([rows_high, rows_low], axis=0)


def folded(product):
    half = product.shape[0] // 2
    return product[:half] + product[half:]


def apply(left, high, low):
    if left.shape[1] <= 128:
        return folded(dot(tall(left), doubled(high, low)))
    left_high, left_low = split(left)
    return folded(dot(jnp.concatenate([left_high, left_low], axis=0), high)) + dot(left_high, low)


def times(left, right):
    return apply(left, *split(right))


def eye(rows, columns):
    shape = (rows, columns)
    return lax.broadcasted_iota(jnp.int32, shape, 0) == lax.broadcasted_iota(jnp.int32, shape, 1)


def upper_inverses(grams, base):
    spread = grams[0].shape[0]
    diagonal = eye(spread, spread)
    above = lax.broadcasted_iota(jnp.int32, (spread, spread), 0) < lax.broadcasted_iota(
        jnp.int32, (spread, spread), 1
    )
    halves = [jnp.where(diagonal, 0.5 * gram, 0.0) for gram in grams]
    columns = [jnp.sum(half, axis=0, keepdims=True) for half in halves]
    scaled = [
        jnp.where(above, gram, 0.0) / jnp.sum(half, axis=1, keepdims=True)
        for gram, half in zip(grams, halves)
    ]

    def owner(size):
        return lax.broadcasted_iota(jnp.int32, (size, spread), 1) // size

    def compact(value, size, row=lambda block: block):
        owns = owner(size)
        result = value[row(0) * size : (row(0) + 1) * size]
        for block in range(1, spread // size):
            at = row(block) * size
            result = jnp.where(owns == block, value[at : at + size], result)
        return result

    def expanded(value, size, row=lambda block: block):
        owns = owner(size)
        masks = [(owns == block).astype(BF16) for block in range(spread // size)]
        terms = []
        for term in split(value):
            rows = [jnp.zeros_like(term)] * (spread // size)
            for block, mask in enumerate(masks):
                if row(block) is not None:
                    rows[row(block)] = term * mask
            terms.append(jnp.concatenate(rows, axis=0))
        return doubled(*terms)

    size = base
    unit = compact(diagonal.astype(F32), size)
    powers = [compact(value, size) for value in scaled]
    results = [unit - power for power in powers]
    rights = [expanded(power, size) for power in powers]
    powers = [folded(dot(tall(power), right)) for power, right in zip(powers, rights)]
    reach = 2
    while reach < size:
        reach *= 2
        rights = [expanded(power, size) for power in powers]
        if reach < size:
            lefts = [jnp.concatenate([r, p], axis=0) for r, p in zip(results, powers)]
        else:
            lefts = results
        products = [folded(dot(tall(left), right)) for left, right in zip(lefts, rights)]
        results = [result + product[:size] for result, product in zip(results, products)]
        if reach < size:
            powers = [product[size:] for product in products]
    while size < spread:
        odd = lax.rem(owner(size), 2) == 1
        edges = [
            jnp.where(odd, compact(value, size, lambda block: block & ~1), 0.0) for value in scaled
        ]
        rights = [expanded(result, size) for result in results]
        products = [folded(dot(tall(edge), right)) for edge, right in zip(edges, rights)]
        rights = [
            expanded(product, size, lambda block: block - 1 if block & 1 else None)
            for product in products
        ]
        products = [folded(dot(tall(result), right)) for result, right in zip(results, rights)]
        results = [
            jnp.concatenate(
                [jnp.where(odd, -product, result), jnp.where(odd, result, 0.0)], axis=0
            )
            for result, product in zip(results, products)
        ]
        size *= 2
    return [result / column for result, column in zip(results, columns)]


def reflectors(values, active):
    double, spread = values[0].shape
    pairs = [wide(value) for value in values]
    grams = [dot(pair, pair, TN) for pair in pairs]
    grams = [
        (g[:spread, :spread] + g[spread:, spread:]) + (g[:spread, spread:] + g[spread:, :spread])
        for g in grams
    ]
    triangles = upper_inverses(grams, 16 if len(values) > 8 else 32)
    unit = eye(double, double).astype(F32)
    scaled = []
    for pair, triangle in zip(pairs, triangles):
        high, low = split(triangle)
        right = jnp.concatenate(
            [jnp.concatenate([high, high], axis=1), jnp.concatenate([low, low], axis=1)], axis=0
        )
        product = dot(pair, right, NT)
        scaled.append(product[:, :spread] + product[:, spread:])
    for pair, value, kept in zip(pairs, scaled, active):
        if kept is not True:
            value = jnp.where(kept, value, 0.0)
        yield split(unit - folded(dot(tall(value), pair, NT)))


def runs_of(slots, extra=0):
    size = next(size for size in (4, 2, 1) if slots % size == 0)
    bounds = [0, 1] + list(range(size, slots + 1, size)) if size > 1 else list(range(slots + 1))
    runs = list(zip(bounds[:-1], bounds[1:]))
    runs[-1] = (runs[-1][0], runs[-1][1] + extra)
    return runs


def edges_kernel(source, kept, last, first):
    last[...] = source[:, source.shape[1] - 1]
    first[...] = source[0, :2]


def reflect_kernel(sweeps, last_slot, source, *refs):
    count, double, spread = source.shape[1:]
    found = [refs[i * 8 : i * 8 + 8] for i in range(len(sweeps))]
    limit = last_slot - lax.axis_index("row") * count
    values = [source[sweep, b] for sweep in sweeps for b in range(count)]
    active = [b < count - 2 or b <= limit for _ in sweeps for b in range(count)]
    for i, (high, low) in enumerate(reflectors(values, active)):
        found[i // count][0][i % count] = high
        found[i // count][1][i % count] = low
    runs = runs_of(count, 1)[1:]
    state = [[None] * len(runs) for _ in found]
    maps = [[None] * len(runs) for _ in found]
    for step in range(max(stop - at for at, stop in runs)):
        for j, (at, stop) in enumerate(runs):
            if at + step >= stop:
                continue
            for i, (k_high, k_low, q_high, q_low, _, _, _, beyond) in enumerate(found):
                b = at + step - 1
                high, low = k_high[b, :spread, :], k_low[b, :spread, :]
                if step == 0:
                    both = high.astype(F32) + low.astype(F32)
                else:
                    both = apply(state[i][j], high, low)
                state[i][j] = both[:, spread:]
                q_high[b], q_low[b] = split(both[:, :spread])
                if b == count - 2 or (at + step + 1 == stop and b < count - 1):
                    maps[i][j] = both[:, spread:]
                if b == count - 1:
                    beyond[...] = both[:, spread:]
    for each, (_, _, _, _, join_high, join_low, upto, _) in zip(maps, found):
        spans = {(j, j + 1): value for j, value in enumerate(each)}
        length = 2
        while length <= len(runs):
            half = 1 << ((length - 1).bit_length() - 1)
            for j in range(len(runs) - length + 1):
                spans[j, j + length] = times(spans[j, j + half], spans[j + half, j + length])
            length += 1
        for j in range(len(runs)):
            upto[j] = spans[0, j + 1]
            for stop in range(len(runs)):
                block = spans.get((j, stop + 1), jnp.zeros((spread, spread), F32))
                rows, columns = (slice(i * spread, (i + 1) * spread) for i in (j, stop))
                join_high[rows, columns], join_low[rows, columns] = split(block)


def reflect(refl_v, sweeps):
    slots, double, spread = refl_v.shape[1:]
    runs = len(runs_of(slots)) - 1
    shape = jax.ShapeDtypeStruct
    shapes = [shape((slots, double, double), BF16)] * 2
    shapes += [shape((slots, spread, spread), BF16)] * 2
    shapes += [shape((runs * spread, runs * spread), BF16)] * 2
    shapes += [shape((runs, spread, spread), F32), shape((spread, spread), F32)]
    results = whole_call(
        functools.partial(reflect_kernel, sweeps, lax.axis_size("row") * slots - 3),
        shapes * len(sweeps), len(sweeps) * slots * 300_000_000, [], [refl_v], vmem=24,
    )
    return [results[i * 8 : i * 8 + 8] for i in range(len(sweeps))]


def edge_kernel(
    count, last_slot, left, right, upto1, upto2, beyond, left_high, left_low, right_high, right_low,
    q_high, q_low, reach, total,
):
    sweeps, _, spread = left.shape
    extra = right.shape[0]
    first = lax.axis_index("row") * count
    values = [left[i] for i in range(sweeps)] + [right[i] for i in range(extra)]
    active = [(first > 0) & (first - 1 <= last_slot)] * sweeps
    active += [first + count + i <= last_slot for i in range(extra)]
    for i, (high, low) in enumerate(reflectors(values, active)):
        if i < sweeps:
            left_high[i], left_low[i] = high, low
        else:
            right_high[i - sweeps], right_low[i - sweeps] = high, low
    state = beyond[...]
    for i in range(extra):
        both = apply(state, right_high[i, :spread, :], right_low[i, :spread, :])
        q_high[i], q_low[i] = split(both[:, :spread])
        state = both[:, spread:]
    for i, upto in enumerate((upto1, upto2)):
        entry = left_high[i, :spread, spread:].astype(F32) + left_low[i, :spread, spread:].astype(F32)
        reach[i, 0] = entry
        for j in range(upto.shape[0] - 1):
            reach[i, j + 1] = times(entry, upto[j])
        total[i] = times(entry, upto[upto.shape[0] - 1])


def merge_kernel(owners, cauchy, *refs):
    pieces, (merged, chosen) = refs[:-2], refs[-2:]
    rows, columns = pieces[0].shape
    mine = lax.axis_index("col")
    chosen[...] = rolled(cauchy[...], mine * rows)[:, : chosen.shape[1]]
    left = [
        chosen[pl.ds(pl.multiple_of((mine ^ owner) * rows, rows), rows), :rows] for owner in owners
    ]
    left_high, left_low = split(jnp.concatenate(left, axis=0))
    step = columns // 4
    for part in range(4):
        at = slice(part * step, (part + 1) * step)
        right_high, right_low = split(jnp.concatenate([piece[:, at] for piece in pieces], axis=0))
        merged[:, at] = dot(left_high, right_high, TN) + (
            dot(left_high, right_low, TN) + dot(left_low, right_high, TN)
        )


def shifted(array, by):
    devices = lax.axis_size("row")
    return lax.ppermute(array, "row", [(i, (i + by) % devices) for i in range(devices)])


def swapped(array, axis, distance):
    devices = lax.axis_size(axis)
    return lax.ppermute(array, axis, [(i, i ^ distance) for i in range(devices)])


def after_all(array, *others):
    return lax.optimization_barrier((array, *others))[0]


def rolled(value, left):
    width = value.shape[1]
    return pltpu.roll(value, lax.rem(width - left, width), 1)


def slot_table(left, own, right=None):
    (left_ref, at), extra = left, 0 if right is None else right.shape[0]
    table = [(left_ref, at)] + [(own, b) for b in range(own.shape[0])]
    return table + [(right, b) for b in range(extra)]


def chain(aligned, k_high, k_low, runs, join_high, join_low, slots, y_local, joins):
    rows, spread = joins.shape[1:]
    carry = [jnp.zeros((rows, spread), F32)] * len(runs)

    def advance(j, slot):
        fresh = aligned[:, slot * spread : (slot + 1) * spread]
        (high, b), (low, _) = k_high[slot], k_low[slot]
        both = apply(jnp.concatenate([carry[j], fresh], axis=1), high[b], low[b])
        y_local[slot] = both[:, :spread]
        carry[j] = both[:, spread:]

    for step in range(max(min(stop, slots) - at for at, stop in runs)):
        for j, (at, stop) in enumerate(runs):
            if at + step < min(stop, slots):
                advance(j, at + step)
    beyond = list(range(slots, runs[-1][1]))
    added = apply(jnp.concatenate(carry[:-1], axis=1), join_high[...], join_low[...])
    joins[0], joins[1] = jnp.zeros_like(carry[0]), carry[0]
    entered = [added[:, j * spread : (j + 1) * spread] + carry[j + 1] for j in range(len(runs) - 1)]
    for j, value in enumerate(entered[:-1]):
        joins[j + 2] = value
    for slot in beyond:
        advance(len(runs) - 1, slot)
    return entered[-1]


def terms(table, runs):
    return [jnp.concatenate([ref[b] for ref, b in table[at:stop]], axis=1) for at, stop in runs]


def settled(runs, joins, q_high, q_low, y_local, line):
    spread = y_local.shape[2]
    highs, lows = terms(q_high, runs[1:]), terms(q_low, runs[1:])
    for j, (at, stop) in enumerate(runs):
        added = apply(joins[j], highs[j - 1], lows[j - 1]) if j else None
        for slot in range(at, stop):
            value = y_local[slot]
            if j:
                value = value + added[:, (slot - at) * spread : (slot - at + 1) * spread]
            line[:, slot * spread : (slot + 1) * spread] = value


def reached(runs, entry, reach, q_high, q_low, line):
    spread = entry.shape[0]
    line[:, :spread] = entry
    highs, lows = terms(q_high, runs[1:]), terms(q_low, runs[1:])
    for j, (at, stop) in enumerate(runs[1:]):
        line[:, at * spread : stop * spread] = apply(reach[j], highs[j], lows[j])


def first_kernel(
    count, start, home, after, left_high, left_low, k_high, k_low, right_high, right_low, join_high,
    join_low, q_high, q_low, q_right_high, q_right_low, line, state, y_local, joins,
):
    spread = state.shape[1]
    offset = start[0]
    aligned = rolled(jnp.concatenate([home[...], after[...]], axis=1), offset)
    runs = runs_of(count, y_local.shape[0] - count)
    highs = slot_table((left_high, 0), k_high, right_high)
    lows = slot_table((left_low, 0), k_low, right_low)
    state[...] = chain(aligned, highs, lows, runs, join_high, join_low, count, y_local, joins)
    q_highs = slot_table((None, 0), q_high, q_right_high)
    q_lows = slot_table((None, 0), q_low, q_right_low)
    settled(runs, joins, q_highs, q_lows, y_local, line)

    @pl.when(lax.axis_index("row") == 0)
    def _():
        line[:, :spread] = pltpu.roll(home[:, :spread], lax.rem(spread - offset, spread), 1)


def second_kernel(
    count, start, line, state_in, left_high, left_low, k_high, k_low, join_high, join_low, y_local,
    joins, state, head,
):
    spread = head.shape[1]
    ahead = start[1] - start[0]
    aligned = rolled(line[...], ahead + spread)
    runs = runs_of(count, y_local.shape[0] - count)
    highs, lows = slot_table((left_high, 1), k_high), slot_table((left_low, 1), k_low)
    state[:, spread:] = chain(
        aligned, highs, lows, runs, join_high, join_low, count, y_local, joins
    )
    state[:, :spread] = state_in[...]
    head[...] = pltpu.roll(
        line[:, : 2 * spread], lax.rem(4 * spread - ahead, 2 * spread), 1
    )[:, :spread]


def base_kernel(count, start, head, joins, y_local, q_high, q_low, base, line):
    spread = head.shape[1]
    runs = runs_of(count, y_local.shape[0] - count)
    q_highs, q_lows = slot_table((None, 0), q_high), slot_table((None, 0), q_low)
    settled(runs, joins, q_highs, q_lows, y_local, line)

    @pl.when(lax.axis_index("row") == 0)
    def _():
        line[:, :spread] = head[...]

    base[...] = rolled(line[...], spread - start[1])[:, : base.shape[1]]


def response_kernel(
    count, start, q_high, q_low, q_right_high, q_right_low, reach, left_high, left_low, k_high,
    k_low, join_high, join_low, totals, y_local, joins, through_device, line,
):
    spread = line.shape[0]
    entry = left_high[0, :spread, :spread].astype(F32) + left_low[0, :spread, :spread].astype(F32)
    q_highs = slot_table((None, 0), q_high, q_right_high)
    q_lows = slot_table((None, 0), q_low, q_right_low)
    reached(runs_of(count, line.shape[1] // spread - count), entry, reach.at[0], q_highs, q_lows, line)
    aligned = rolled(line[...], start[1] - start[0] + spread)
    runs = runs_of(count, y_local.shape[0] - count)
    highs, lows = slot_table((left_high, 1), k_high), slot_table((left_low, 1), k_low)
    through_device[1] = chain(
        aligned, highs, lows, runs, join_high, join_low, count, y_local, joins
    )
    through_device[0], through_device[2] = totals[0], totals[1]


def moved_home(start, line, high, low):
    spread, columns = high.shape
    high[...], low[...] = split(rolled(line[...], spread - start[1])[:, :columns])


def home_first_kernel(count, start, joins, y_local, q_high, q_low, high, low, line):
    runs = runs_of(count, y_local.shape[0] - count)
    q_highs, q_lows = slot_table((None, 0), q_high), slot_table((None, 0), q_low)
    settled(runs, joins, q_highs, q_lows, y_local, line)
    moved_home(start, line, high, low)


def home_second_kernel(count, start, reach, q_high, q_low, left_high, left_low, high, low, line):
    spread = line.shape[0]
    entry = left_high[1, :spread, :spread].astype(F32) + left_low[1, :spread, :spread].astype(F32)
    q_highs, q_lows = slot_table((None, 0), q_high), slot_table((None, 0), q_low)
    reached(runs_of(count, 1), entry, reach.at[1], q_highs, q_lows, line)
    moved_home(start, line, high, low)


def is_upper(level):
    return lax.rem(lax.axis_index("row") // (1 << level), 2) == 1


def through(states, maps):
    spread = maps.shape[1]
    first, second = states[:, :spread], states[:, spread:]
    return jnp.concatenate(
        [times(first, maps[0]), times(first, maps[1]) + times(second, maps[2])], axis=1
    )


def join_maps_kernel(level, *refs):
    upper = is_upper(level)
    mine, other, refs = refs[0], refs[1], list(refs[2:])
    inner = refs.pop(0) if level else None
    high, inside, *both = refs
    spread = high.shape[1]
    low = [jnp.where(upper, other[i], mine[i]) for i in range(3)]
    for i in range(3):
        high[i] = jnp.where(upper, mine[i], other[i])

    def joined(later):
        return [
            times(low[0], later[0]),
            times(low[0], later[1]) + times(low[1], later[2]),
            times(low[2], later[2]),
        ]

    if both:
        for i, value in enumerate(joined(high)):
            both[0][i] = value
    if level:
        for i, value in enumerate(joined(inner)):
            inside[i] = jnp.where(upper, value, inner[i])
    else:
        unit = eye(spread, spread).astype(F32)
        for i, value in enumerate([unit, jnp.zeros_like(unit), unit]):
            inside[i] = jnp.where(upper, low[i], value)


def join_states_kernel(level, mine, other, high, *refs):
    upper = is_upper(level)
    if level:
        inner, before, refs = refs[0], refs[1], refs[2:]
    low = jnp.where(upper, other[...], mine[...])
    refs[0][...] = through(low, high) + jnp.where(upper, mine[...], other[...])
    if level:
        refs[1][...] = before[...] + jnp.where(upper, through(low, inner), 0.0)
    else:
        refs[1][...] = jnp.where(upper, low, 0.0)


def final_kernel(
    levels, half, inner, before, base, high_first, high_second, low_first, low_second, out
):
    enters = jnp.where(is_upper(levels - 1), half[...], 0.0)
    incoming = before[...] + through(enters, inner)
    high = jnp.concatenate([high_first[...], high_second[...]], axis=0)
    low = jnp.concatenate([low_first[...], low_second[...]], axis=0)
    out[...] = base[...] + apply(incoming, high, low)


def whole_call(kernel, shapes, flops, scalars, arrays, scratch=(), vmem=8, aliases={}):
    return pl.pallas_call(
        kernel,
        out_shape=shapes,
        in_specs=[SMEM] * len(scalars) + [VMEM] * len(arrays),
        out_specs=jax.tree.map(lambda shape: VMEM, shapes),
        scratch_shapes=list(scratch),
        input_output_aliases=aliases,
        compiler_params=pltpu.CompilerParams(vmem_limit_bytes=vmem << 20),
        cost_estimate=pl.CostEstimate(
            flops=flops, bytes_accessed=4_000_000, transcendentals=0
        ),
    )(*scalars, *arrays)


def shards(panel, cauchy, refl_v, block_start):
    rows, columns = panel.shape
    slots, _, spread = refl_v.shape[1:]
    levels = lax.axis_size("row").bit_length() - 1
    last_slot = lax.axis_size("row") * slots - 3
    shape = functools.partial(jax.ShapeDtypeStruct, dtype=F32)
    starts = [block_start]
    count, runs = lax.axis_size("col"), len(runs_of(slots))
    square = (spread, spread)

    pieces, owners = [panel], [0]
    distance = count // 2
    while distance:
        pieces += [swapped(piece, "col", distance) for piece in pieces]
        if owners == [0]:
            pair = shape((2,) + refl_v.shape[2:])
            refl_v, left, right = whole_call(
                edges_kernel, [shape(refl_v.shape), pair, pair], 10_000_000, [], [refl_v],
                aliases={0: 0},
            )
            left, right = shifted(left, 1), shifted(right, -1)
            if slots <= 16:
                one, two = reflect(refl_v, (0, 1))
            else:
                [one], [two] = reflect(refl_v, (0,)), reflect(refl_v, (1,))
            high1, low1, qh1, ql1, *joins1, upto1, beyond = one
            high2, low2, qh2, ql2, *joins2, upto2, _ = two
            pieces = list(lax.optimization_barrier((*pieces, beyond, left, right))[:2])
        owners += [owner ^ distance for owner in owners]
        distance //= 2
    k_pair = jax.ShapeDtypeStruct((2,) + (2 * spread, 2 * spread), BF16)
    q_pair = jax.ShapeDtypeStruct((2,) + square, BF16)
    lh, ll, rh, rl, qrh, qrl, reach, totals = whole_call(
        functools.partial(edge_kernel, slots, last_slot),
        [k_pair] * 4 + [q_pair] * 2 + [shape((2, runs - 1) + square), shape((2,) + square)],
        2_000_000_000, [], [left, right, upto1, upto2, beyond],
    )
    pieces[0] = after_all(pieces[0], totals)
    merged = whole_call(
        functools.partial(merge_kernel, owners), shape((rows, columns)),
        1_000_000_000, [], [cauchy] + pieces,
        [pltpu.VMEM((cauchy.shape[0], 128 * pl.cdiv(rows, 128)), F32)],
    )
    after = shifted(merged[:, : 4 * spread], -1)

    y_response, joins_response, maps = whole_call(
        functools.partial(response_kernel, slots),
        [shape((slots + 1,) + square), shape((runs,) + square), shape((3,) + square)],
        4_000_000_000, starts,
        [qh1, ql1, qrh, qrl, after_all(reach, merged), lh, ll, high2, low2, *joins2,
         totals],
        [pltpu.VMEM((spread, columns + 3 * spread), F32)],
    )
    line, state1 = whole_call(
        functools.partial(first_kernel, slots),
        [shape((rows, columns + 3 * spread)), shape((rows, spread))], 3_000_000_000, starts,
        [after_all(merged, maps), after, lh, ll, high1, low1, rh, rl, *joins1, qh1, ql1, qrh, qrl],
        [pltpu.VMEM((slots + 3, rows, spread), F32), pltpu.VMEM((runs, rows, spread), F32)],
    )
    states = shape((rows, 2 * spread))
    y2, entries2, state, head2 = whole_call(
        functools.partial(second_kernel, slots),
        [shape((slots + 1, rows, spread)), shape((runs, rows, spread)), states,
         shape((rows, spread))],
        3_000_000_000, starts,
        [line, state1, lh, ll, high2, low2, *joins2],
    )
    groups, inside, enters = [], None, None
    for level in range(levels - 1):
        other, state_other = swapped(maps, "row", 1 << level), swapped(state, "row", 1 << level)
        if level == 0:
            other = after_all(other, state)
        if level == levels - 2:
            base = whole_call(
                functools.partial(base_kernel, slots), shape((rows, columns)), 2_000_000_000, starts,
                [after_all(head2, state), entries2, y2, qh2, ql2],
                [pltpu.VMEM((rows, columns + spread), F32)],
            )
            other = after_all(other, base)
        high, inner, *maps = whole_call(
            functools.partial(join_maps_kernel, level),
            [shape((3,) + square)] * (2 if level == levels - 2 else 3), 400_000_000, [],
            [maps, other] + ([inside] if level else []),
        )
        maps = maps[0] if maps else None
        if level == 0:
            home = jax.ShapeDtypeStruct((spread, columns), BF16)
            home_line = pltpu.VMEM((spread, columns + spread), F32)
            high_second, low_second = whole_call(
                functools.partial(home_second_kernel, slots), [home, home], 3_000_000_000, starts,
                [after_all(reach, high), qh2, ql2, lh, ll], [home_line],
            )
        arrays = [state, state_other, high] + ([inside, enters] if level else [])
        state, enters = whole_call(
            functools.partial(join_states_kernel, level), [states] * 2, 100_000_000, [], arrays,
        )
        inside = inner
    half = swapped(state, "row", 1 << (levels - 1))
    high_first, low_first = whole_call(
        functools.partial(home_first_kernel, slots), [home, home], 1_500_000_000, starts,
        [after_all(joins_response, state), y_response, qh2, ql2], [home_line],
    )
    return whole_call(
        functools.partial(final_kernel, levels), shape((rows, columns)), 1_000_000_000, [],
        [half, inside, enters, base, high_first, high_second, low_first, low_second],
    )


def solution(mesh):
    placed = (P("col", "row"), P(), P(None, "row", None, None), P())
    return jax.shard_map(
        shards, mesh=mesh, in_specs=placed, out_specs=P("col", "row"), check_vma=False
    )
```
